128 devices in a mesh: pts: 16 (over x, z), comp: 8 (over y, core).
Axes of the slice: x: 4, y: 4, z: 4, core: 2. Of those that a mesh axis runs over, the one named last changes fastest.
Arguments:
- spectrum: float32 [1152, 16384], P(None, ('pts', 'comp')), may hold values from 0.05 to 4
- turning: float32 [1152, 16384], P(None, ('pts', 'comp')), may hold values from -0.45 to 0.45
- courant_x: float32 [1152, 16384], P(('pts', 'comp')), may hold values from -0.45 to 0.45
- courant_y: float32 [1152, 16384], P(('pts', 'comp')), may hold values from -0.45 to 0.45
- neighbors: int32 [4, 16384], replicated, may hold values from 0 to 16383, as said below
- nest_spectra: float32 [13312, 1152], P(('pts', 'comp')), may hold values from 0.05 to 4
- nest_owner: int32 [13312, 1], P(('pts', 'comp')), may hold values from 0 to 127; in each aligned block of 104 rows (0 to 103, 104 to 207, ...) at most 4 rows name the same one
- nest_point: int32 [13312], P(('pts', 'comp')), may hold values from 0 to 127, as said below
- nest_weight: float32 [13312], P(('pts', 'comp')), may hold values from 0.02 to 1
Outputs:
- spectrum_next: float32 [1152, 16384], P(None, ('pts', 'comp'))
The draws below stay inside these ranges and needn't reach their ends.
Inputs may be any that keep to these rules, and one draw needn't show every extreme that they name: `neighbors`: rows are the west, east, south and north neighbours of each sea point on a grid 128 points wide in point order, or the point itself where the neighbour is land or outside. `nest_owner`: among the rows of one device no owner is named more than 4 times. `nest_point`: each row names the west or the east end of its owner's grid row: 0 or 127.
All inputs are finite; a program needn't handle non-finite values.
Results may differ from the reference program's by a relative error of at most 0.0003.
Values sent between devices are 32-bit elements; how exact they have to be, the bound alone decides.
A program may use at most 64 MiB of HBM per device.

```python
import math
import jax
import jax.numpy as jnp
import numpy as np

NTH = 36
NK = 32
PTS_DEV = 128
NB_DEV = 104
CAP = 4
REF_SUB = 2
ADV_SUB = 3
GRIDW = 128
COMPS = 1152
POINTS = 16384
NB = 13312
N_PTS = 16
N_COMP = 8


def draw_neighbors(key, part):
    key = jax.random.fold_in(key, 11)
    position = jnp.arange(POINTS, dtype=jnp.int32)
    column = position % GRIDW
    west_side = jnp.where(column > 0, position - 1, position)
    east_side = jnp.where(column < GRIDW - 1, position + 1, position)
    south_side = jnp.where(position >= GRIDW, position - GRIDW, position)
    north_side = jnp.where(position < POINTS - GRIDW, position + GRIDW, position)
    sides = jnp.stack([west_side, east_side, south_side, north_side], axis=0)
    land_mask = jax.random.randint(key, (4, POINTS), 0, 10) == 0
    return jnp.where(land_mask, position[None, :], sides).astype(jnp.int32)


def draw_nest_point(key, part):
    key = jax.random.fold_in(key, 23)
    which_end = jax.random.randint(key, (NB,), 0, 2)
    return (which_end * (PTS_DEV - 1)).astype(jnp.int32)


def block_scale(key, shape, shards, least, high):
    loudness = 1.0
    for dim, parts in shards:
        steps = jax.random.uniform(jax.random.fold_in(jax.random.fold_in(key, 6), dim), (parts,), jnp.float32, least / len(shards), high / len(shards))
        loudness = loudness * jnp.repeat(jnp.exp(steps), shape[dim] // parts).reshape((-1,) + (1,) * (len(shape) - 1 - dim))
    return loudness


def deal_out(rng, own, number, rows, amount, top, most, slope):
    sequence = jax.random.permutation(rng, amount)
    packed, usual = load_shares(amount, rows * top, most, slope, True), load_shares(amount, rows * top, most, slope, False)
    places = jnp.arange(amount)

    def named(tallies, rotation):
        used = int((tallies > 0).sum())
        fixed = max(1, used // 4)
        passed = fixed + (places - fixed + rotation * (used - fixed)) % max(1, amount - fixed)
        return jnp.zeros((amount,), jnp.int32).at[sequence[jnp.where(places < fixed, places, passed)]].set(jnp.asarray(tallies, jnp.int32))

    tallies = jnp.where(number % 4 == 0, named(packed, number // 4), named(usual, number - number // 4 - 1))
    mixed = jax.random.permutation(jax.random.fold_in(own, 3), amount)
    donor, receiver = mixed[0:amount // 2 * 2:2], mixed[1:amount // 2 * 2:2]
    room = jnp.minimum(tallies[donor] - 1, most - tallies[receiver]) // 2
    room = jnp.where((donor == sequence[0]) | (receiver == sequence[0]) | (tallies[receiver] == 0), 0, jnp.maximum(room, 0))
    passed = jax.random.randint(jax.random.fold_in(own, 4), (amount // 2,), 0, 1 << 20) % (room + 1)
    tallies = tallies.at[donor].add(-passed).at[receiver].add(passed)
    members = jnp.searchsorted(jnp.cumsum(tallies), jnp.arange(rows * top), side="right").astype(jnp.int32)
    table = members.reshape(top, rows).T
    table = table[jax.random.permutation(jax.random.fold_in(own, 1), rows)]
    rotation = jax.random.randint(jax.random.fold_in(own, 2), (rows, 1), 0, top)
    return jnp.take_along_axis(table, (jnp.arange(top)[None, :] + rotation) % top, axis=1)


def load_shares(number_of, total, reach, lean, full):
    loads = [(1 << 20) // math.isqrt(rank ** lean) + 1 for rank in range(1, number_of + 1)]
    largest = reach if full else min(reach, max(-(-total // number_of), total * loads[0] // sum(loads)))
    least = 1 if total - largest >= number_of - 1 else 0
    counts, spare = [largest] + [least] * (number_of - 1), total - largest - least * (number_of - 1)
    while spare > 0:
        free = [i for i in range(1, number_of) if counts[i] < largest] or [i for i in range(1, number_of) if counts[i] < reach]
        whole, left = sum([loads[i] for i in free]), spare
        for i in free:
            extra = min(reach - counts[i], max(1, left * loads[i] // whole), spare)
            counts[i] = counts[i] + extra
            spare = spare - extra
    return np.array(counts)


def setup_inputs(seed: int = 0) -> dict:
    splits = jax.random.split(jax.random.key(seed), 10)
    spectrum = jnp.clip(jnp.exp(math.log(4.0) - 4.3820266 * jax.random.uniform(splits[0], (COMPS, POINTS), jnp.float32) ** block_scale(splits[0], (COMPS, POINTS), ((1, 128),), -0.2, 0.2)), 0.05, 4.0)
    turning = jnp.clip(jax.random.uniform(splits[1], (COMPS, POINTS), jnp.float32, -0.45, 0.45) * block_scale(splits[1], (COMPS, POINTS), ((1, 128),), -0.4, 0.0), -0.45, 0.45)
    courant_x = jnp.clip(jax.random.uniform(splits[2], (COMPS, POINTS), jnp.float32, -0.45, 0.45) * block_scale(splits[2], (COMPS, POINTS), ((0, 128),), -0.4, 0.0), -0.45, 0.45)
    courant_y = jnp.clip(jax.random.uniform(splits[3], (COMPS, POINTS), jnp.float32, -0.45, 0.45) * block_scale(splits[3], (COMPS, POINTS), ((0, 128),), -0.4, 0.0), -0.45, 0.45)
    neighbors = draw_neighbors(jax.random.fold_in(splits[9], 71), 0)
    nest_spectra = jnp.clip(jnp.exp(math.log(4.0) - 4.3820266 * jax.random.uniform(splits[5], (NB, COMPS), jnp.float32) ** block_scale(splits[5], (NB, COMPS), ((0, 128),), -0.2, 0.2)), 0.05, 4.0)
    nest_owner_keys = jax.random.split(jax.random.fold_in(splits[6], 1), NB // NB_DEV)
    nest_owner_turns = jax.random.permutation(jax.random.fold_in(splits[6], 3), NB // NB_DEV)
    nest_owner = jax.vmap(lambda own, number: deal_out(jax.random.fold_in(splits[6], 2), own, number, NB_DEV, N_PTS * N_COMP, 1, CAP, 2))(nest_owner_keys, nest_owner_turns).reshape((NB, 1))
    nest_point = draw_nest_point(jax.random.fold_in(splits[9], 71), 0)
    nest_weight = jnp.clip(jnp.exp(math.log(1.0) - 3.912023 * jax.random.uniform(splits[8], (NB,), jnp.float32) ** block_scale(splits[8], (NB,), ((0, 128),), -0.2, 0.2)), 0.02, 1.0)
    return {"spectrum": spectrum, "turning": turning, "courant_x": courant_x, "courant_y": courant_y, "neighbors": neighbors, "nest_spectra": nest_spectra, "nest_owner": nest_owner, "nest_point": nest_point, "nest_weight": nest_weight}


def refract(energy, rates):
    upstream = jnp.roll(energy, -1, axis=1)
    fluxes = jnp.maximum(rates, 0.0) * energy + jnp.minimum(rates, 0.0) * upstream
    return energy - fluxes + jnp.roll(fluxes, 1, axis=1)


def advect(energy, speed_x, speed_y, upwind_x, upwind_y):
    from_x = jnp.take_along_axis(energy, upwind_x, axis=1)
    from_y = jnp.take_along_axis(energy, upwind_y, axis=1)
    return energy - jnp.abs(speed_x) * (energy - from_x) - jnp.abs(speed_y) * (energy - from_y)


def reference(spectrum, turning, courant_x, courant_y, neighbors, nest_spectra, nest_owner, nest_point, nest_weight):
    cube_shape = (NK, NTH, POINTS)
    energy = spectrum.reshape(cube_shape)
    rates = turning.reshape(cube_shape)
    for substep in range(REF_SUB):
        energy = refract(energy, rates)
    energy = energy.reshape(COMPS, POINTS)
    upwind_x = jnp.where(courant_x > 0, neighbors[0][None, :], neighbors[1][None, :]).astype(jnp.int32)
    upwind_y = jnp.where(courant_y > 0, neighbors[2][None, :], neighbors[3][None, :]).astype(jnp.int32)
    for substep in range(ADV_SUB):
        energy = advect(energy, courant_x, courant_y, upwind_x, upwind_y)
    target = (nest_owner[:, 0] * PTS_DEV + nest_point).astype(jnp.int32)
    weighted = nest_spectra * nest_weight[:, None]
    total_weight = jnp.zeros((POINTS,), jnp.float32).at[target].add(nest_weight)
    added_energy = jnp.zeros((COMPS, POINTS), jnp.float32).at[:, target].add(weighted.T)
    return (energy + added_energy) / (1.0 + total_weight)[None, :]
```

```python
import functools

import jax
import jax.numpy as jnp
from jax import lax
from jax.experimental import pallas as pl
from jax.experimental.pallas import tpu as pltpu
from jax.sharding import PartitionSpec as P

MESH = pl.DeviceIdType.MESH
NTH = 36
CAP = 4
REF_SUB = 2
ADV_SUB = 3
PAD = 16
DMA = pltpu.SemaphoreType.DMA
CHUNKS = ((0, 9),)


def away(at, step):
    return (at + step * (1 - 2 * (at % 2)) + 4) % 4


def peer(i, pts, comp):
    x, z, y, core = pts // 4, pts % 4, comp // 2, comp % 2
    to_x, to_z = away(x, i // 32), away(z, (i // 8) % 4)
    to_y, to_core = away(y, (i // 2) % 4), (core + i) % 2
    return to_x * 4 + to_z, to_y * 2 + to_core


def refract(x, r, tmp, send):
    @pl.loop(0, x.shape[0] // (8 * NTH))
    def _(group):
        base = pl.multiple_of(group * (8 * NTH), 8)

        def substep(load, store):
            def flux(d):
                rate = r[pl.ds(base + d, 8, stride=NTH), :]
                return jnp.maximum(rate, 0.0) * load(d) + jnp.minimum(rate, 0.0) * load((d + 1) % NTH)

            before = flux(NTH - 1)
            for d in range(NTH):
                now = flux(d)
                store(d, load(d) - now + before)
                before = now

        def load_x(d):
            return x[pl.ds(base + d, 8, stride=NTH), :]

        def store_tmp(d, v):
            tmp[pl.ds(8 * d, 8), :] = v

        def load_tmp(d):
            return tmp[pl.ds(8 * d, 8), :]

        def store_send(d, v):
            send[pl.ds(base + d, 8, stride=NTH), :] = v

        substep(load_x, store_tmp)
        substep(load_tmp, store_send)


def prepare(cx, cy, nb, ax, ay, chunk):
    first, n = chunk
    width = 128
    lane = lax.broadcasted_iota(jnp.int32, (4, width), 1)
    side = lax.broadcasted_iota(jnp.int32, (4, width), 0)
    shift = jnp.where(side == 0, -1, jnp.where(side == 1, 1, jnp.where(side == 2, -width, width)))

    @pl.loop(0, nb.shape[1] // (8 * width))
    def _(group):
        base = pl.multiple_of(group * (8 * n), 8)
        for j in range(8):
            columns = pl.ds(pl.multiple_of((group * 8 + j) * width, width), width)
            there = (nb[:, columns] == lane + shift + (group * 8 + j) * width).astype(jnp.float32)
            for c, a, low in ((cx, ax, 0), (cy, ay, 2)):
                v = c[pl.ds(first, n), columns]
                a[pl.ds(base + j * n, n), :] = v * jnp.where(v > 0, there[low : low + 1], there[low + 1 : low + 2])


def advect(src, src_at, dst, dst_at, ax, ay, n):
    rows = ax.shape[0]

    def one(row):
        e = src[pl.ds(src_at + row, 8), :]
        south = src[pl.ds(src_at + row - n, 8), :]
        north = src[pl.ds(src_at + row + n, 8), :]
        west, east = pltpu.roll(e, 1, 1), pltpu.roll(e, 127, 1)
        vx, vy = ax[pl.ds(row, 8), :], ay[pl.ds(row, 8), :]
        out = e - jnp.abs(vx) * (e - jnp.where(vx > 0, west, east))
        dst[pl.ds(dst_at + row, 8), :] = out - jnp.abs(vy) * (e - jnp.where(vy > 0, south, north))

    @pl.loop(0, rows // 64)
    def _(step):
        for j in range(8):
            one(pl.multiple_of(step * 64, 8) + 8 * j)


def kernel(x_hbm, r_hbm, cx_hbm, cy_hbm, nb_hbm, out, x, r, cx, cy, nb, tmp, send, *rest):
    nc = len(CHUNKS)
    bufs, (in_sem, own_sem, send_sem, recv_sem) = rest[:-4], rest[-4:]
    recvs, axs, ays, g1s, g2s, backs = (bufs[i * nc : (i + 1) * nc] for i in range(6))
    pts, comp = lax.axis_index("pts"), lax.axis_index("comp")
    me = pts * 8 + comp
    devices = 128
    loads = [
        pltpu.make_async_copy(a, b, in_sem.at[i])
        for i, (a, b) in enumerate(((x_hbm, x), (r_hbm, r), (cx_hbm, cx), (cy_hbm, cy), (nb_hbm, nb)))
    ]
    for c in loads:
        c.start()
    barrier = pltpu.get_barrier_semaphore()

    @pl.loop(1, devices)
    def _(i):
        pl.semaphore_signal(barrier, inc=1, device_id=peer(i, pts, comp), device_id_type=MESH)

    for ref in (*recvs, *g1s, *g2s):
        ref[pl.ds(0, PAD), :] = jnp.zeros((PAD, 128), jnp.float32)
        ref[pl.ds(ref.shape[0] - PAD, PAD), :] = jnp.zeros((PAD, 128), jnp.float32)
    loads[0].wait()
    loads[1].wait()
    refract(x, r, tmp, send)
    pl.semaphore_wait(barrier, devices - 1)

    for j, (first, n) in enumerate(CHUNKS):

        @pl.loop(1, devices)
        def _(i):
            p, c = peer(devices - i, pts, comp)
            to = p * 8 + c
            pltpu.make_async_remote_copy(
                send.at[pl.ds(to * 9 + first, n)],
                recvs[j].at[pl.ds(PAD + me * n, n)],
                send_sem.at[j],
                recv_sem.at[j],
                device_id=(p, c),
                device_id_type=MESH,
            ).start()

        pltpu.make_async_copy(
            send.at[pl.ds(me * 9 + first, n)], recvs[j].at[pl.ds(PAD + me * n, n)], own_sem.at[j]
        ).start()
    for c in loads[2:]:
        c.wait()
    for j, chunk in enumerate(CHUNKS):
        prepare(cx, cy, nb, axs[j], ays[j], chunk)
    for j, (first, n) in enumerate(CHUNKS):
        arrived = recvs[j].at[pl.ds(0, (devices - 1) * n)]
        pltpu.make_async_copy(
            send.at[pl.ds(me * 9 + first, n)], recvs[j].at[pl.ds(PAD + me * n, n)], own_sem.at[j]
        ).wait()
        w = pltpu.make_async_remote_copy(
            arrived, arrived, send_sem.at[j], recv_sem.at[j], device_id=(pts, comp), device_id_type=MESH
        )
        w.wait_recv()
        advect(recvs[j], PAD, g1s[j], PAD, axs[j], ays[j], n)
        advect(g1s[j], PAD, g2s[j], PAD, axs[j], ays[j], n)
        advect(g2s[j], PAD, backs[j], 0, axs[j], ays[j], n)

        @pl.loop(1, devices)
        def _(i):
            p, c = peer(devices - i, pts, comp)
            to = p * 8 + c
            pltpu.make_async_remote_copy(
                backs[j].at[pl.ds(to * n, n)],
                out.at[pl.ds(me * 9 + first, n)],
                send_sem.at[nc + j],
                recv_sem.at[nc + j],
                device_id=(p, c),
                device_id_type=MESH,
            ).start()

        pltpu.make_async_copy(
            backs[j].at[pl.ds(me * n, n)], out.at[pl.ds(me * 9 + first, n)], own_sem.at[nc + j]
        ).start()
    for j, (first, n) in enumerate(CHUNKS):
        pltpu.make_async_copy(
            backs[j].at[pl.ds(me * n, n)], out.at[pl.ds(me * 9 + first, n)], own_sem.at[nc + j]
        ).wait()
        arrived = recvs[j].at[pl.ds(0, (devices - 1) * n)]
        for h in range(2):
            w = pltpu.make_async_remote_copy(
                arrived, arrived, send_sem.at[h * nc + j], recv_sem.at[h * nc + j], device_id=(pts, comp), device_id_type=MESH
            )
            w.wait_send()
            if h == 1:
                w.wait_recv()


def propagate(spectrum, turning, courant_x, courant_y, neighbors):
    f32 = jnp.float32
    any_ = pl.BlockSpec(memory_space=pl.ANY)
    per = [n * 128 for _, n in CHUNKS]
    padded = [pltpu.VMEM((rows + 2 * PAD, 128), f32) for rows in per]
    plain = [pltpu.VMEM((rows, 128), f32) for rows in per]
    nc = len(CHUNKS)
    return pl.pallas_call(
        kernel,
        out_shape=jax.ShapeDtypeStruct((1152, 128), f32),
        in_specs=[any_] * 5,
        out_specs=any_,
        scratch_shapes=[
            pltpu.VMEM((1152, 128), f32),
            pltpu.VMEM((1152, 128), f32),
            pltpu.VMEM((9, 16384), f32),
            pltpu.VMEM((9, 16384), f32),
            pltpu.VMEM((4, 16384), jnp.int32),
            pltpu.VMEM((8 * NTH, 128), f32),
            pltpu.VMEM((1152, 128), f32),
            *padded, *plain, *plain, *padded, *padded, *plain,
            DMA((5,)),
            DMA((2 * nc,)),
            DMA((2 * nc,)),
            DMA((2 * nc,)),
        ],
        name="propagate",
        compiler_params=pltpu.CompilerParams(
            collective_id=1, has_side_effects=True, vmem_limit_bytes=48 * 1024 * 1024
        ),
    )(spectrum, turning, courant_x, courant_y, neighbors)


def body(spectrum, turning, courant_x, courant_y, neighbors, nest_spectra, nest_owner, nest_point, nest_weight):
    point_count = spectrum.shape[1]
    devices = 128
    row_count = nest_spectra.shape[0]
    energy = propagate(spectrum, turning, courant_x, courant_y, neighbors)
    weighted = nest_spectra * nest_weight[:, None]
    owner_ids = nest_owner[:, 0]
    row_index = jnp.arange(row_count, dtype=jnp.int32)
    same_owner = owner_ids[:, None] == owner_ids[None, :]
    earlier = jnp.logical_and(same_owner, row_index[None, :] < row_index[:, None])
    rank_index = jnp.sum(earlier.astype(jnp.int32), axis=1)
    slot_index = owner_ids * CAP + rank_index
    slot_count = devices * CAP
    slot_table = (jnp.arange(slot_count, dtype=jnp.int32)[:, None] == slot_index[None, :]).astype(jnp.float32)
    packed = jnp.dot(slot_table, weighted, precision=lax.Precision.HIGHEST)
    packed_weight = jnp.dot(slot_table, nest_weight, precision=lax.Precision.HIGHEST)
    packed_point = jnp.dot(slot_table, nest_point.astype(jnp.float32), precision=lax.Precision.HIGHEST)
    got_rows, got_weight, got_point = (
        lax.all_to_all(packed, ("pts", "comp"), split_axis=0, concat_axis=0, tiled=True),
        lax.all_to_all(packed_weight, ("pts", "comp"), split_axis=0, concat_axis=0, tiled=True),
        lax.all_to_all(packed_point, ("pts", "comp"), split_axis=0, concat_axis=0, tiled=True),
    )
    point_table = (
        got_point.astype(jnp.int32)[:, None] == jnp.arange(point_count, dtype=jnp.int32)[None, :]
    ).astype(jnp.float32)
    added_energy = lax.dot_general(got_rows, point_table, (((0,), (0,)), ((), ())), precision=lax.Precision.HIGHEST)
    total_weight = jnp.dot(got_weight, point_table, precision=lax.Precision.HIGHEST)
    return (energy + added_energy) / (1.0 + total_weight)[None, :]


def solution(mesh):
    placed = (
        P(None, ("pts", "comp")),
        P(None, ("pts", "comp")),
        P(("pts", "comp"), None),
        P(("pts", "comp"), None),
        P(),
        P(("pts", "comp"), None),
        P(("pts", "comp"), None),
        P(("pts", "comp")),
        P(("pts", "comp")),
    )
    return jax.shard_map(body, mesh=mesh, in_specs=placed, out_specs=P(None, ("pts", "comp")), check_vma=False)
```

```python
import functools

import jax
import jax.numpy as jnp
from jax import lax
from jax.experimental import pallas as pl
from jax.experimental.pallas import tpu as pltpu
from jax.sharding import PartitionSpec as P

MESH = pl.DeviceIdType.MESH
DMA = pltpu.SemaphoreType.DMA
F32 = jnp.float32
BF16 = jnp.bfloat16
NTH = 36
DEVICES = 128
WIDTH = 128
COMPS = 1152
OWN = 9
PAD = 16
STEPS = 136
UNROLL = 7
PARTS = ((0, 4, 5, (3, 1)), (4, 3, 1, (5, 3)), (7, 3, 3, (5, 1)))


def at(device):
    return dict(device_id=(device // 8, device % 8), device_id_type=MESH)


def digit(index, bit):
    return (index >> bit) & 3


def each_peer(body):
    def some(j, carry):
        for q in range(UNROLL):
            body(DEVICES - 1 - (j * UNROLL + q))
        return carry

    whole = (DEVICES - 1) // UNROLL
    lax.fori_loop(0, whole, some, 0)
    for i in range(DEVICES - 1 - whole * UNROLL, 0, -1):
        body(i)


def far_first(i):
    high, low = i & 0b1010100, i & 0b0101010
    return (low << 1) | ((high >> 1) ^ low) | (i & 1)


def refract(x, r, tmp, send):
    @pl.loop(0, x.shape[0] // (8 * NTH))
    def _(group):
        base = pl.multiple_of(group * (8 * NTH), 8)

        def substep(load, store):
            def flux(d):
                rate = r[pl.ds(base + d, 8, stride=NTH), :]
                return jnp.maximum(rate, 0.0) * load(d) + jnp.minimum(rate, 0.0) * load((d + 1) % NTH)

            before = flux(NTH - 1)
            for d in range(NTH):
                now = flux(d)
                store(d, load(d) - now + before)
                before = now

        def load_x(d):
            return x[pl.ds(base + d, 8, stride=NTH), :]

        def store_tmp(d, v):
            tmp[pl.ds(8 * d, 8), :] = v

        def load_tmp(d):
            return tmp[pl.ds(8 * d, 8), :]

        def store_send(d, v):
            send[pl.ds(base + d, 8, stride=NTH), :] = v

        substep(load_x, store_tmp)
        substep(load_tmp, store_send)


def local_sums(spectra, owner, point, weight, sums):
    rows = spectra.shape[0]
    w = weight[...]
    diagonal = lax.broadcasted_iota(jnp.int32, (rows, rows), 0) == lax.broadcasted_iota(jnp.int32, (rows, rows), 1)
    w_column = jnp.sum(jnp.where(diagonal, w, 0.0), axis=1, keepdims=True)
    o = owner[...]
    end = (point[...] > 0).astype(jnp.int32)
    place = lax.broadcasted_iota(jnp.int32, (256, rows), 0)
    for (first, tiles, bit, (b1, b2)), out in zip(PARTS, sums):
        target = (o & 1) * 128 + digit(o, bit) * 32 + digit(o, b1) * 8 + digit(o, b2) * 2 + end
        table = (place == target).astype(F32).astype(BF16)
        for t in range(tiles):
            if first + t < COMPS // WIDTH:
                v = spectra[:, (first + t) * WIDTH : (first + t + 1) * WIDTH] * w_column
            else:
                v = jnp.broadcast_to(w_column, (rows, WIDTH))
            high = v.astype(BF16)
            low = (v - high.astype(F32)).astype(BF16)
            out[:, t * WIDTH : (t + 1) * WIDTH] = jnp.dot(table, high, preferred_element_type=F32) + jnp.dot(
                table, low, preferred_element_type=F32
            )


def prepare(cx, cy, nb, axa, aya, axb, ayb):
    lane = lax.broadcasted_iota(jnp.int32, (4, WIDTH), 1)
    side = lax.broadcasted_iota(jnp.int32, (4, WIDTH), 0)
    shift = lane + jnp.where(side == 0, -1, jnp.where(side == 1, 1, jnp.where(side == 2, -WIDTH, WIDTH)))
    for a in (axa, aya):
        a[pl.ds(0, 16), :] = jnp.zeros((16, WIDTH), F32)
        a[pl.ds(16 + 8 * DEVICES, 8 * (STEPS - DEVICES)), :] = jnp.zeros((8 * (STEPS - DEVICES), WIDTH), F32)

    @pl.loop(0, DEVICES // 8)
    def _(group):
        for j in range(8):
            s = group * 8 + j
            columns = pl.ds(pl.multiple_of(s * WIDTH, WIDTH), WIDTH)
            there = (nb[:, columns] == shift + s * WIDTH).astype(F32)
            for c, a, b, low in ((cx, axa, axb, 0), (cy, aya, ayb, 2)):
                up, down = there[low : low + 1], there[low + 1 : low + 2]
                v = c[pl.ds(0, 8), columns]
                a[pl.ds(pl.multiple_of((s + 2) * 8, 8), 8), :] = v * jnp.where(v > 0, up, down)
                v = c[pl.ds(8, 1), columns]
                b[pl.ds(pl.multiple_of(group * 8, 8) + j, 1), :] = v * jnp.where(v > 0, up, down)


def upwind(e, south, north, vx, vy):
    west, east = pltpu.roll(e, 1, 1), pltpu.roll(e, WIDTH - 1, 1)
    out = e - jnp.abs(vx) * (e - jnp.where(vx > 0, west, east))
    return out - jnp.abs(vy) * (e - jnp.where(vy > 0, south, north))


def advect(recv, back, axa, aya, axb, ayb):
    zero = jnp.zeros((8, WIDTH), F32)

    def steps(group, carry):
        e0m, e0, e1m, e1, e2m, e2, x1, y1, x2, y2 = carry
        base = pl.multiple_of(group * 72, 8)
        courant = pl.multiple_of(group * 64, 8)
        for j in range(8):
            e0p = recv[pl.ds(base + (PAD + 9 * (j + 1)), 8), :]
            x0 = axa[pl.ds(courant + 8 * (j + 2), 8), :]
            y0 = aya[pl.ds(courant + 8 * (j + 2), 8), :]
            e1p = upwind(e0, e0m, e0p, x0, y0)
            e2p = upwind(e1, e1m, e1p, x1, y1)
            back[pl.ds(base + (24 + 9 * (j - 2)), 8), :] = upwind(e2, e2m, e2p, x2, y2)
            e0m, e0, e1m, e1, e2m, e2 = e0, e0p, e1, e1p, e2, e2p
            x2, y2, x1, y1 = x1, y1, x0, y0
        return e0m, e0, e1m, e1, e2m, e2, x1, y1, x2, y2

    lax.fori_loop(0, STEPS // 8, steps, (zero, recv[pl.ds(PAD, 8), :]) + (zero,) * 8)
    groups = DEVICES // 8
    e = [recv[pl.ds(PAD + 8 + 72 * g, 8, stride=OWN), :] for g in range(groups)]
    row = lax.broadcasted_iota(jnp.int32, (8, WIDTH), 0)
    for _ in range(3):
        up = [pltpu.roll(v, 1, 0) for v in e]
        down = [pltpu.roll(v, 7, 0) for v in e]
        e = [
            upwind(
                e[g],
                jnp.where(row == 0, up[g - 1], up[g]),
                jnp.where(row == 7, down[(g + 1) % groups], down[g]),
                axb[pl.ds(8 * g, 8), :],
                ayb[pl.ds(8 * g, 8), :],
            )
            for g in range(groups)
        ]
    for g in range(groups):
        back[pl.ds(24 + 8 + 72 * g, 8, stride=OWN), :] = e[g]


def kernel(
    x_hbm, r_hbm, cx_hbm, cy_hbm, nb_hbm, ns_hbm, owner_hbm, point_hbm, weight_hbm, out, added_hbm, scale_hbm, *scratch
):
    x, r, cx, cy, nb, ns, owner, point, weight = scratch[:9]
    tmp, send, recv, back, axa, aya, axb, ayb, added, scale = scratch[9:19]
    sums, pair, chip, first_in, second_out, second_in = (scratch[19 + 3 * i : 22 + 3 * i] for i in range(6))
    in_sem, own_sem, send_sem, recv_sem, result_sem, part_send, part_recv = scratch[37:]
    me = lax.axis_index("pts") * 8 + lax.axis_index("comp")
    loads = [
        pltpu.make_async_copy(a, b, in_sem.at[i])
        for i, (a, b) in enumerate(
            (
                (x_hbm, x),
                (r_hbm, r),
                (ns_hbm, ns),
                (owner_hbm, owner),
                (point_hbm, point),
                (weight_hbm, weight),
                (cx_hbm, cx),
                (cy_hbm, cy),
                (nb_hbm, nb),
            )
        )
    ]
    for c in loads:
        c.start()
    barrier = pltpu.get_barrier_semaphore()
    each_peer(lambda i: pl.semaphore_signal(barrier, inc=1, **at(me ^ i)))

    recv[pl.ds(0, PAD), :] = jnp.zeros((PAD, WIDTH), F32)
    tail = recv.shape[0] - PAD - COMPS
    recv[pl.ds(PAD + COMPS, tail), :] = jnp.zeros((tail, WIDTH), F32)
    loads[0].wait()
    loads[1].wait()
    refract(x, r, tmp, send)
    for c in loads[2:6]:
        c.wait()
    local_sums(ns, owner, point, weight, sums)
    pl.semaphore_wait(barrier, DEVICES - 1)

    def over(stage, p, ref, source, target, device):
        return pltpu.make_async_remote_copy(source, target, part_send.at[stage, p], part_recv.at[stage, p], **at(device))

    def wait_part(stage, p, ref):
        w = over(stage, p, ref, ref, ref, me)
        w.wait_recv()
        w.wait_send()

    for p in range(3):
        other = pl.ds(pl.multiple_of((1 - me % 2) * 128, 128), 128)
        over(0, p, None, sums[p].at[other], pair[p], me ^ 1).start()

    def transpose(stage, source, target, source_at, target_at):
        def start(i):
            to = me ^ far_first(i)
            pltpu.make_async_remote_copy(
                source.at[pl.ds(source_at + to * OWN, OWN)],
                target.at[pl.ds(target_at + me * OWN, OWN)],
                send_sem.at[stage],
                recv_sem.at[stage],
                **at(to),
            ).start()

        each_peer(start)
        own = pltpu.make_async_copy(
            source.at[pl.ds(source_at + me * OWN, OWN)], target.at[pl.ds(target_at + me * OWN, OWN)], own_sem.at[stage]
        )
        own.start()
        rest = recv.at[pl.ds(0, (DEVICES - 1) * OWN)]
        return own, pltpu.make_async_remote_copy(rest, rest, send_sem.at[stage], recv_sem.at[stage], **at(me))

    own, moved = transpose(0, send, recv, 0, PAD)

    for p, (first, tiles, bit, _) in enumerate(PARTS):
        wait_part(0, p, pair[p])
        mine = pl.ds(pl.multiple_of((me % 2) * 128, 128), 128)
        chip[p][...] = sums[p][mine, :] + pair[p][...]
        for d in range(1, 4):
            to = me ^ (d << bit)
            block = pl.ds(pl.multiple_of(digit(to, bit) * 32, 32), 32)
            over(1, p, None, chip[p].at[block], first_in[p].at[pl.ds((d - 1) * 32, 32)], to).start()

    for c in loads[6:]:
        c.wait()
    prepare(cx, cy, nb, axa, aya, axb, ayb)
    own.wait()
    moved.wait_recv()
    advect(recv, back, axa, aya, axb, ayb)
    own2, moved2 = transpose(1, back, out, 24, 0)

    for p, (first, tiles, bit, (b1, b2)) in enumerate(PARTS):
        wait_part(1, p, first_in[p])
        block = pl.ds(pl.multiple_of(digit(me, bit) * 32, 32), 32)
        for t in range(4):
            if t < tiles:
                lanes = slice(t * WIDTH, (t + 1) * WIDTH)
                v = chip[p][block, lanes]
                for d in range(3):
                    v = v + first_in[p][d * 32 : (d + 1) * 32, lanes]
            else:
                v = jnp.zeros((32, WIDTH), F32)
            second_out[p][pl.ds(t, 32, stride=4), :] = v

        @pl.loop(1, 16)
        def _(q):
            to = me ^ (((q >> 2) << b1) | ((q & 3) << b2))
            block = digit(to, b1) * 4 + digit(to, b2)
            over(
                2,
                p,
                None,
                second_out[p].at[pl.ds(pl.multiple_of(block * 8, 8), 8)],
                second_in[p].at[pl.ds(pl.multiple_of(q * 8, 8), 8)],
                to,
            ).start()

    lane = lax.broadcasted_iota(jnp.int32, (WIDTH, WIDTH), 1)
    for p, (first, tiles, bit, (b1, b2)) in enumerate(PARTS):
        wait_part(2, p, second_in[p].at[pl.ds(8, 120)])
        block = digit(me, b1) * 4 + digit(me, b2)
        v = second_out[p][pl.ds(pl.multiple_of(block * 8, 8), 8), :]
        for q in range(1, 16):
            v = v + second_in[p][pl.ds(8 * q, 8), :]
        columns = v.T
        for t in range(tiles):
            if first + t < COMPS // WIDTH:
                added[pl.ds((first + t) * WIDTH, WIDTH), :] = jnp.where(
                    lane == 0, columns[:, t : t + 1], jnp.where(lane == WIDTH - 1, columns[:, 4 + t : 5 + t], 0.0)
                )
            else:
                one = lax.broadcasted_iota(jnp.int32, (8, WIDTH), 1)
                total = jnp.where(one == 0, v[t : t + 1], jnp.where(one == WIDTH - 1, v[4 + t : 5 + t], 0.0))
                scale[...] = 1.0 / (1.0 + total)
    results = [
        pltpu.make_async_copy(added, added_hbm, result_sem.at[0]),
        pltpu.make_async_copy(scale, scale_hbm, result_sem.at[1]),
    ]
    for c in results:
        c.start()
    moved.wait_send()
    for c in results:
        c.wait()
    own2.wait()
    moved2.wait_send()
    moved2.wait_recv()


def timestep(*arrays):
    whole = [pltpu.VMEM(a.shape, a.dtype) for a in arrays]
    anywhere = pl.BlockSpec(memory_space=pl.ANY)

    def rows(n):
        return pltpu.VMEM((n, WIDTH), F32)

    def parts(n):
        return [pltpu.VMEM((n, tiles * WIDTH), F32) for _, tiles, _, _ in PARTS]

    return pl.pallas_call(
        kernel,
        out_shape=(
            jax.ShapeDtypeStruct((COMPS, WIDTH), F32),
            jax.ShapeDtypeStruct((COMPS, WIDTH), F32),
            jax.ShapeDtypeStruct((8, WIDTH), F32),
        ),
        in_specs=[anywhere] * 9,
        out_specs=(anywhere,) * 3,
        scratch_shapes=[
            *whole,
            rows(8 * NTH),
            rows(COMPS),
            rows(PAD + OWN * (STEPS + 2)),
            rows(24 + OWN * STEPS),
            rows(8 * (STEPS + 2)),
            rows(8 * (STEPS + 2)),
            rows(DEVICES),
            rows(DEVICES),
            rows(COMPS),
            rows(8),
            *parts(256),
            *parts(128),
            *parts(128),
            *parts(96),
            *[rows(128) for _ in PARTS],
            *[rows(128) for _ in PARTS],
            DMA((9,)),
            DMA((2,)),
            DMA((2,)),
            DMA((2,)),
            DMA((2,)),
            DMA((3, 3)),
            DMA((3, 3)),
        ],
        name="timestep",
        compiler_params=pltpu.CompilerParams(
            collective_id=1, has_side_effects=True, vmem_limit_bytes=48 * 1024 * 1024
        ),
    )(*arrays)


def body(spectrum, turning, courant_x, courant_y, neighbors, nest_spectra, nest_owner, nest_point, nest_weight):
    rows = nest_spectra.shape[0]
    energy, added, scale = timestep(
        spectrum,
        turning,
        courant_x,
        courant_y,
        neighbors,
        nest_spectra,
        nest_owner.reshape(1, rows),
        nest_point.reshape(1, rows),
        nest_weight.reshape(1, rows),
    )
    return (energy + added) * scale[0:1, :]


def solution(mesh):
    placed = (
        P(None, ("pts", "comp")),
        P(None, ("pts", "comp")),
        P(("pts", "comp"), None),
        P(("pts", "comp"), None),
        P(),
        P(("pts", "comp"), None),
        P(("pts", "comp"), None),
        P(("pts", "comp")),
        P(("pts", "comp")),
    )
    return jax.shard_map(body, mesh=mesh, in_specs=placed, out_specs=P(None, ("pts", "comp")), check_vma=False)
```

```python
import functools

import jax
import jax.numpy as jnp
from jax import lax
from jax.experimental import pallas as pl
from jax.experimental.pallas import tpu as pltpu
from jax.sharding import PartitionSpec as P

MESH = pl.DeviceIdType.MESH
DMA = pltpu.SemaphoreType.DMA
F32 = jnp.float32
BF16 = jnp.bfloat16
NTH = 36
DEVICES = 128
WIDTH = 128
COMPS = 1152
OWN = 9
PAD = 16
STEPS = 136
UNROLL = 127
PARTS = ((0, 4, 5, (3, 1)), (4, 3, 1, (5, 3)), (7, 3, 3, (5, 1)))


def at(device):
    return dict(device_id=(device // 8, device % 8), device_id_type=MESH)


def digit(index, bit):
    return (index >> bit) & 3


def each_peer(body):
    def some(j, carry):
        for q in range(UNROLL):
            body(DEVICES - 1 - (j * UNROLL + q))
        return carry

    whole = (DEVICES - 1) // UNROLL
    lax.fori_loop(0, whole, some, 0)
    for i in range(DEVICES - 1 - whole * UNROLL, 0, -1):
        body(i)


def far_first(i):
    high, low = i & 0b1010100, i & 0b0101010
    return (low << 1) | ((high >> 1) ^ low) | (i & 1)


def refract(x, r, tmp, send):
    @pl.loop(0, x.shape[0] // (8 * NTH))
    def _(group):
        base = pl.multiple_of(group * (8 * NTH), 8)

        def substep(load, store):
            def flux(d):
                rate = r[pl.ds(base + d, 8, stride=NTH), :]
                return jnp.maximum(rate, 0.0) * load(d) + jnp.minimum(rate, 0.0) * load((d + 1) % NTH)

            before = flux(NTH - 1)
            for d in range(NTH):
                now = flux(d)
                store(d, load(d) - now + before)
                before = now

        def load_x(d):
            return x[pl.ds(base + d, 8, stride=NTH), :]

        def store_tmp(d, v):
            tmp[pl.ds(8 * d, 8), :] = v

        def load_tmp(d):
            return tmp[pl.ds(8 * d, 8), :]

        def store_send(d, v):
            send[pl.ds(base + d, 8, stride=NTH), :] = v

        substep(load_x, store_tmp)
        substep(load_tmp, store_send)


def local_sums(spectra, owner, point, weight, sums):
    rows = spectra.shape[0]
    w = weight[...]
    diagonal = lax.broadcasted_iota(jnp.int32, (rows, rows), 0) == lax.broadcasted_iota(jnp.int32, (rows, rows), 1)
    w_column = jnp.sum(jnp.where(diagonal, w, 0.0), axis=1, keepdims=True)
    o = owner[...]
    end = (point[...] > 0).astype(jnp.int32)
    place = lax.broadcasted_iota(jnp.int32, (256, rows), 0)
    for (first, tiles, bit, (b1, b2)), out in zip(PARTS, sums):
        target = (o & 1) * 128 + digit(o, bit) * 32 + digit(o, b1) * 8 + digit(o, b2) * 2 + end
        table = (place == target).astype(F32).astype(BF16)
        for t in range(tiles):
            if first + t < COMPS // WIDTH:
                v = spectra[:, (first + t) * WIDTH : (first + t + 1) * WIDTH] * w_column
            else:
                v = jnp.broadcast_to(w_column, (rows, WIDTH))
            high = v.astype(BF16)
            low = (v - high.astype(F32)).astype(BF16)
            out[:, t * WIDTH : (t + 1) * WIDTH] = jnp.dot(table, high, preferred_element_type=F32) + jnp.dot(
                table, low, preferred_element_type=F32
            )


def prepare(cx, cy, nb, axa, aya, axb, ayb):
    lane = lax.broadcasted_iota(jnp.int32, (4, WIDTH), 1)
    side = lax.broadcasted_iota(jnp.int32, (4, WIDTH), 0)
    shift = lane + jnp.where(side == 0, -1, jnp.where(side == 1, 1, jnp.where(side == 2, -WIDTH, WIDTH)))
    for a in (axa, aya):
        a[pl.ds(0, 16), :] = jnp.zeros((16, WIDTH), F32)
        a[pl.ds(16 + 8 * DEVICES, 8 * (STEPS - DEVICES)), :] = jnp.zeros((8 * (STEPS - DEVICES), WIDTH), F32)

    @pl.loop(0, DEVICES // 8)
    def _(group):
        for j in range(8):
            s = group * 8 + j
            columns = pl.ds(pl.multiple_of(s * WIDTH, WIDTH), WIDTH)
            there = (nb[:, columns] == shift + s * WIDTH).astype(F32)
            for c, a, b, low in ((cx, axa, axb, 0), (cy, aya, ayb, 2)):
                up, down = there[low : low + 1], there[low + 1 : low + 2]
                v = c[pl.ds(0, 8), columns]
                a[pl.ds(pl.multiple_of((s + 2) * 8, 8), 8), :] = v * jnp.where(v > 0, up, down)
                v = c[pl.ds(8, 1), columns]
                b[pl.ds(pl.multiple_of(group * 8, 8) + j, 1), :] = v * jnp.where(v > 0, up, down)


def upwind(e, south, north, vx, vy):
    west, east = pltpu.roll(e, 1, 1), pltpu.roll(e, WIDTH - 1, 1)
    out = e - jnp.abs(vx) * (e - jnp.where(vx > 0, west, east))
    return out - jnp.abs(vy) * (e - jnp.where(vy > 0, south, north))


def advect(recv, back, axa, aya, axb, ayb):
    zero = jnp.zeros((8, WIDTH), F32)

    def steps(group, carry):
        e0m, e0, e1m, e1, e2m, e2, x1, y1, x2, y2 = carry
        base = pl.multiple_of(group * 1224, 8)
        courant = pl.multiple_of(group * 1088, 8)
        for j in range(136):
            e0p = recv[pl.ds(base + (PAD + 9 * (j + 1)), 8), :]
            x0 = axa[pl.ds(courant + 8 * (j + 2), 8), :]
            y0 = aya[pl.ds(courant + 8 * (j + 2), 8), :]
            e1p = upwind(e0, e0m, e0p, x0, y0)
            e2p = upwind(e1, e1m, e1p, x1, y1)
            back[pl.ds(base + (24 + 9 * (j - 2)), 8), :] = upwind(e2, e2m, e2p, x2, y2)
            e0m, e0, e1m, e1, e2m, e2 = e0, e0p, e1, e1p, e2, e2p
            x2, y2, x1, y1 = x1, y1, x0, y0
        return e0m, e0, e1m, e1, e2m, e2, x1, y1, x2, y2

    lax.fori_loop(0, STEPS // 136, steps, (zero, recv[pl.ds(PAD, 8), :]) + (zero,) * 8)
    groups = DEVICES // 8
    e = [recv[pl.ds(PAD + 8 + 72 * g, 8, stride=OWN), :] for g in range(groups)]
    row = lax.broadcasted_iota(jnp.int32, (8, WIDTH), 0)
    for _ in range(3):
        up = [pltpu.roll(v, 1, 0) for v in e]
        down = [pltpu.roll(v, 7, 0) for v in e]
        e = [
            upwind(
                e[g],
                jnp.where(row == 0, up[g - 1], up[g]),
                jnp.where(row == 7, down[(g + 1) % groups], down[g]),
                axb[pl.ds(8 * g, 8), :],
                ayb[pl.ds(8 * g, 8), :],
            )
            for g in range(groups)
        ]
    for g in range(groups):
        back[pl.ds(24 + 8 + 72 * g, 8, stride=OWN), :] = e[g]


def kernel(
    x_hbm, r_hbm, cx_hbm, cy_hbm, nb_hbm, ns_hbm, owner_hbm, point_hbm, weight_hbm, out, added, scale, *scratch
):
    x, r, cx, cy, nb, ns, owner, point, weight = scratch[:9]
    tmp, send, recv, back, axa, aya, axb, ayb = scratch[9:17]
    sums, pair, chip, first_in, second_out, second_in = (scratch[17 + 3 * i : 20 + 3 * i] for i in range(6))
    in_sem, own_sem, send_sem, recv_sem, part_send, part_recv = scratch[35:]
    me = lax.axis_index("pts") * 8 + lax.axis_index("comp")
    loads = [
        pltpu.make_async_copy(a, b, in_sem.at[i])
        for i, (a, b) in enumerate(
            (
                (x_hbm, x),
                (r_hbm, r),
                (ns_hbm, ns),
                (owner_hbm, owner),
                (point_hbm, point),
                (weight_hbm, weight),
                (cx_hbm, cx),
                (cy_hbm, cy),
                (nb_hbm, nb),
            )
        )
    ]
    for c in loads:
        c.start()
    barrier = pltpu.get_barrier_semaphore()
    each_peer(lambda i: pl.semaphore_signal(barrier, inc=1, **at(me ^ i)))

    recv[pl.ds(0, PAD), :] = jnp.zeros((PAD, WIDTH), F32)
    tail = recv.shape[0] - PAD - COMPS
    recv[pl.ds(PAD + COMPS, tail), :] = jnp.zeros((tail, WIDTH), F32)
    loads[0].wait()
    loads[1].wait()
    refract(x, r, tmp, send)
    for c in loads[2:6]:
        c.wait()
    local_sums(ns, owner, point, weight, sums)
    pl.semaphore_wait(barrier, DEVICES - 1)

    def over(stage, p, ref, source, target, device):
        return pltpu.make_async_remote_copy(source, target, part_send.at[stage, p], part_recv.at[stage, p], **at(device))

    def wait_part(stage, p, ref):
        w = over(stage, p, ref, ref, ref, me)
        w.wait_recv()
        w.wait_send()

    for p in range(3):
        other = pl.ds(pl.multiple_of((1 - me % 2) * 128, 128), 128)
        over(0, p, None, sums[p].at[other], pair[p], me ^ 1).start()

    def transpose(stage, source, target, source_at, target_at):
        def start(i):
            to = me ^ far_first(i)
            pltpu.make_async_remote_copy(
                source.at[pl.ds(source_at + to * OWN, OWN)],
                target.at[pl.ds(target_at + me * OWN, OWN)],
                send_sem.at[stage],
                recv_sem.at[stage],
                **at(to),
            ).start()

        each_peer(start)
        own = pltpu.make_async_copy(
            source.at[pl.ds(source_at + me * OWN, OWN)], target.at[pl.ds(target_at + me * OWN, OWN)], own_sem.at[stage]
        )
        own.start()
        rest = recv.at[pl.ds(0, (DEVICES - 1) * OWN)]
        return own, pltpu.make_async_remote_copy(rest, rest, send_sem.at[stage], recv_sem.at[stage], **at(me))

    own, moved = transpose(0, send, recv, 0, PAD)

    for p, (first, tiles, bit, _) in enumerate(PARTS):
        wait_part(0, p, pair[p])
        mine = pl.ds(pl.multiple_of((me % 2) * 128, 128), 128)
        chip[p][...] = sums[p][mine, :] + pair[p][...]
        for d in range(1, 4):
            to = me ^ (d << bit)
            block = pl.ds(pl.multiple_of(digit(to, bit) * 32, 32), 32)
            over(1, p, None, chip[p].at[block], first_in[p].at[pl.ds((d - 1) * 32, 32)], to).start()

    for c in loads[6:]:
        c.wait()
    prepare(cx, cy, nb, axa, aya, axb, ayb)
    own.wait()
    moved.wait_recv()
    advect(recv, back, axa, aya, axb, ayb)
    own2, moved2 = transpose(1, back, out, 24, 0)

    for p, (first, tiles, bit, (b1, b2)) in enumerate(PARTS):
        wait_part(1, p, first_in[p])
        block = pl.ds(pl.multiple_of(digit(me, bit) * 32, 32), 32)
        for t in range(4):
            if t < tiles:
                lanes = slice(t * WIDTH, (t + 1) * WIDTH)
                v = chip[p][block, lanes]
                for d in range(3):
                    v = v + first_in[p][d * 32 : (d + 1) * 32, lanes]
            else:
                v = jnp.zeros((32, WIDTH), F32)
            second_out[p][pl.ds(t, 32, stride=4), :] = v

        @pl.loop(1, 16)
        def _(q):
            to = me ^ (((q >> 2) << b1) | ((q & 3) << b2))
            block = digit(to, b1) * 4 + digit(to, b2)
            over(
                2,
                p,
                None,
                second_out[p].at[pl.ds(pl.multiple_of(block * 8, 8), 8)],
                second_in[p].at[pl.ds(pl.multiple_of(q * 8, 8), 8)],
                to,
            ).start()

    lane = lax.broadcasted_iota(jnp.int32, (WIDTH, WIDTH), 1)
    for p, (first, tiles, bit, (b1, b2)) in enumerate(PARTS):
        wait_part(2, p, second_in[p].at[pl.ds(8, 120)])
        block = digit(me, b1) * 4 + digit(me, b2)
        v = second_out[p][pl.ds(pl.multiple_of(block * 8, 8), 8), :]
        for q in range(1, 16):
            v = v + second_in[p][pl.ds(8 * q, 8), :]
        columns = v.T
        for t in range(tiles):
            if first + t < COMPS // WIDTH:
                added[pl.ds((first + t) * WIDTH, WIDTH), :] = jnp.where(
                    lane == 0, columns[:, t : t + 1], jnp.where(lane == WIDTH - 1, columns[:, 4 + t : 5 + t], 0.0)
                )
            else:
                one = lax.broadcasted_iota(jnp.int32, (8, WIDTH), 1)
                total = jnp.where(one == 0, v[t : t + 1], jnp.where(one == WIDTH - 1, v[4 + t : 5 + t], 0.0))
                scale[...] = 1.0 / (1.0 + total)
    moved.wait_send()
    own2.wait()
    moved2.wait_send()
    moved2.wait_recv()


def timestep(*arrays):
    whole = [pltpu.VMEM(a.shape, a.dtype) for a in arrays]
    anywhere = pl.BlockSpec(memory_space=pl.ANY)

    def rows(n):
        return pltpu.VMEM((n, WIDTH), F32)

    def parts(n):
        return [pltpu.VMEM((n, tiles * WIDTH), F32) for _, tiles, _, _ in PARTS]

    return pl.pallas_call(
        kernel,
        out_shape=(rows(COMPS), rows(COMPS), rows(8)),
        in_specs=[anywhere] * 9,
        out_specs=(pl.BlockSpec(memory_space=pltpu.VMEM),) * 3,
        scratch_shapes=[
            *whole,
            rows(8 * NTH),
            rows(COMPS),
            rows(PAD + OWN * (STEPS + 2)),
            rows(24 + OWN * STEPS),
            rows(8 * (STEPS + 2)),
            rows(8 * (STEPS + 2)),
            rows(DEVICES),
            rows(DEVICES),
            *parts(256),
            *parts(128),
            *parts(128),
            *parts(96),
            *[rows(128) for _ in PARTS],
            *[rows(128) for _ in PARTS],
            DMA((9,)),
            DMA((2,)),
            DMA((2,)),
            DMA((2,)),
            DMA((3, 3)),
            DMA((3, 3)),
        ],
        name="timestep",
        compiler_params=pltpu.CompilerParams(
            collective_id=1, has_side_effects=True, vmem_limit_bytes=60 * 1024 * 1024
        ),
    )(*arrays)


def body(spectrum, turning, courant_x, courant_y, neighbors, nest_spectra, nest_owner, nest_point, nest_weight):
    rows = nest_spectra.shape[0]
    energy, added, scale = timestep(
        spectrum,
        turning,
        courant_x,
        courant_y,
        neighbors,
        nest_spectra,
        nest_owner.reshape(1, rows),
        nest_point.reshape(1, rows),
        nest_weight.reshape(1, rows),
    )
    return (energy + added) * scale[0:1, :]


def solution(mesh):
    placed = (
        P(None, ("pts", "comp")),
        P(None, ("pts", "comp")),
        P(("pts", "comp"), None),
        P(("pts", "comp"), None),
        P(),
        P(("pts", "comp"), None),
        P(("pts", "comp"), None),
        P(("pts", "comp")),
        P(("pts", "comp")),
    )
    return jax.shard_map(body, mesh=mesh, in_specs=placed, out_specs=P(None, ("pts", "comp")), check_vma=False)
```

```python
import functools

import jax
import jax.numpy as jnp
from jax import lax
from jax.experimental import pallas as pl
from jax.experimental.pallas import tpu as pltpu
from jax.sharding import PartitionSpec as P

MESH = pl.DeviceIdType.MESH
DMA = pltpu.SemaphoreType.DMA
F32 = jnp.float32
BF16 = jnp.bfloat16
NTH = 36
DEVICES = 128
WIDTH = 128
COMPS = 1152
OWN = 9
PAD = 80
BLOCK = 32
PARTS = ((0, 4, 5, (3, 1)), (4, 3, 1, (5, 3)), (7, 3, 3, (5, 1)))


def at(device):
    return dict(device_id=(device // 8, device % 8), device_id_type=MESH)


def digit(index, bit):
    return (index >> bit) & 3


def refract(x, r, tmp, send):
    @pl.loop(0, x.shape[0] // (8 * NTH))
    def _(group):
        base = pl.multiple_of(group * (8 * NTH), 8)

        def substep(load, store):
            def flux(d):
                rate = r[pl.ds(base + d, 8, stride=NTH), :]
                return jnp.maximum(rate, 0.0) * load(d) + jnp.minimum(rate, 0.0) * load((d + 1) % NTH)

            before = flux(NTH - 1)
            for d in range(NTH):
                now = flux(d)
                store(d, load(d) - now + before)
                before = now

        def load_x(d):
            return x[pl.ds(base + d, 8, stride=NTH), :]

        def store_tmp(d, v):
            tmp[pl.ds(8 * d, 8), :] = v

        def load_tmp(d):
            return tmp[pl.ds(8 * d, 8), :]

        def store_send(d, v):
            send[pl.ds(base + d, 8, stride=NTH), :] = v

        substep(load_x, store_tmp)
        substep(load_tmp, store_send)


def local_sums(spectra, owner, point, weight, sums):
    rows = spectra.shape[0]
    w = weight[...]
    diagonal = lax.broadcasted_iota(jnp.int32, (rows, rows), 0) == lax.broadcasted_iota(jnp.int32, (rows, rows), 1)
    w_column = jnp.sum(jnp.where(diagonal, w, 0.0), axis=1, keepdims=True)
    o = owner[...]
    end = (point[...] > 0).astype(jnp.int32)
    place = lax.broadcasted_iota(jnp.int32, (256, rows), 0)
    for (first, tiles, bit, (b1, b2)), out in zip(PARTS, sums):
        target = (o & 1) * 128 + digit(o, bit) * 32 + digit(o, b1) * 8 + digit(o, b2) * 2 + end
        table = (place == target).astype(F32).astype(BF16)
        for t in range(tiles):
            if first + t < COMPS // WIDTH:
                v = spectra[:, (first + t) * WIDTH : (first + t + 1) * WIDTH] * w_column
            else:
                v = jnp.broadcast_to(w_column, (rows, WIDTH))
            high = v.astype(BF16)
            low = (v - high.astype(F32)).astype(BF16)
            out[:, t * WIDTH : (t + 1) * WIDTH] = jnp.dot(table, high, preferred_element_type=F32) + jnp.dot(
                table, low, preferred_element_type=F32
            )


def prepare(cx, cy, nb, axa, aya, axb, ayb):
    lane = lax.broadcasted_iota(jnp.int32, (4, WIDTH), 1)
    side = lax.broadcasted_iota(jnp.int32, (4, WIDTH), 0)
    shift = lane + jnp.where(side == 0, -1, jnp.where(side == 1, 1, jnp.where(side == 2, -WIDTH, WIDTH)))
    for a, edge in ((axa, 16), (aya, 16), (axb, 8), (ayb, 8)):
        a[pl.ds(0, edge), :] = jnp.zeros((edge, WIDTH), F32)
        a[pl.ds(a.shape[0] - edge, edge), :] = jnp.zeros((edge, WIDTH), F32)

    @pl.loop(0, DEVICES // 8)
    def _(group):
        for j in range(8):
            s = group * 8 + j
            columns = pl.ds(pl.multiple_of(s * WIDTH, WIDTH), WIDTH)
            there = (nb[:, columns] == shift + s * WIDTH).astype(F32)
            for c, a, b, low in ((cx, axa, axb, 0), (cy, aya, ayb, 2)):
                up, down = there[low : low + 1], there[low + 1 : low + 2]
                v = c[pl.ds(0, 8), columns]
                a[pl.ds(pl.multiple_of((s + 2) * 8, 8), 8), :] = v * jnp.where(v > 0, up, down)
                v = c[pl.ds(8, 1), columns]
                b[pl.ds(pl.multiple_of(group * 8, 8) + (8 + j), 1), :] = v * jnp.where(v > 0, up, down)


def upwind(e, south, north, vx, vy):
    west, east = pltpu.roll(e, 1, 1), pltpu.roll(e, WIDTH - 1, 1)
    out = e - jnp.abs(vx) * (e - jnp.where(vx > 0, west, east))
    return out - jnp.abs(vy) * (e - jnp.where(vy > 0, south, north))


def advect(block, recv, back, axa, aya, axb, ayb):
    base = pl.multiple_of(block * (BLOCK * OWN), 8)
    low = pl.multiple_of(block * (BLOCK * 8), 8)

    def courants(s):
        rows = pl.ds(low + 8 * (s + 2), 8)
        return axa[rows, :], aya[rows, :]

    def first(s):
        return recv[pl.ds(base + (PAD + OWN * s), 8), :]

    e0, e1, e2, c = {-3: first(-3), -2: first(-2)}, {}, {}, {}
    for s in range(-2, BLOCK + 2):
        e0[s + 1], c[s] = first(s + 1), courants(s)
        e1[s] = upwind(e0[s], e0[s - 1], e0[s + 1], *c[s])
        if s >= 0:
            e2[s - 1] = upwind(e1[s - 1], e1[s - 2], e1[s], *c[s - 1])
        if s >= 2:
            back[pl.ds(base + OWN * (s - 2), 8), :] = upwind(e2[s - 2], e2[s - 3], e2[s - 1], *c[s - 2])
    groups = BLOCK // 8 + 2
    last = groups - 1
    e = [recv[pl.ds(base + (PAD + 8 + 72 * (g - 1)), 8, stride=OWN), :] for g in range(groups)]
    courant = pl.multiple_of(block * BLOCK, 8)
    row = lax.broadcasted_iota(jnp.int32, (8, WIDTH), 0)
    for _ in range(3):
        up = [pltpu.roll(v, 1, 0) for v in e]
        down = [pltpu.roll(v, 7, 0) for v in e]
        e = [
            upwind(
                e[g],
                jnp.where(row == 0, up[max(g - 1, 0)], up[g]),
                jnp.where(row == 7, down[min(g + 1, last)], down[g]),
                axb[pl.ds(courant + 8 * g, 8), :],
                ayb[pl.ds(courant + 8 * g, 8), :],
            )
            for g in range(groups)
        ]
    for g in range(1, last):
        back[pl.ds(base + (8 + 72 * (g - 1)), 8, stride=OWN), :] = e[g]


def kernel(
    x_hbm, r_hbm, cx_hbm, cy_hbm, nb_hbm, ns_hbm, owner_hbm, point_hbm, weight_hbm, out, added, scale, *scratch
):
    spec, r, cx, cy, nb, ns, owner, point, weight = scratch[:9]
    tmp, send, recv, back, axa, aya, axb, ayb = scratch[9:17]
    sums, pair, chip, first_in, second_out, second_in = (scratch[17 + 3 * i : 20 + 3 * i] for i in range(6))
    in_sem, own_sem, send_sem, recv_sem, part_send, part_recv = scratch[35:]
    me = lax.axis_index("pts") * 8 + lax.axis_index("comp")
    loads = [
        pltpu.make_async_copy(a, b, in_sem.at[i])
        for i, (a, b) in enumerate(
            (
                (x_hbm, spec),
                (r_hbm, r),
                (ns_hbm, ns),
                (owner_hbm, owner),
                (point_hbm, point),
                (weight_hbm, weight),
                (cx_hbm, cx),
                (cy_hbm, cy),
                (nb_hbm, nb),
            )
        )
    ]
    for c in loads:
        c.start()
    barrier = pltpu.get_barrier_semaphore()
    for i in range(DEVICES - 1, 0, -1):
        pl.semaphore_signal(barrier, inc=1, **at(me ^ i))

    recv[pl.ds(0, PAD), :] = jnp.zeros((PAD, WIDTH), F32)
    recv[pl.ds(PAD + COMPS, PAD), :] = jnp.zeros((PAD, WIDTH), F32)
    loads[0].wait()
    loads[1].wait()
    refract(spec, r, tmp, send)
    for c in loads[2:6]:
        c.wait()
    local_sums(ns, owner, point, weight, sums)
    pl.semaphore_wait(barrier, DEVICES - 1)

    def over(stage, p, source, target, device):
        return pltpu.make_async_remote_copy(source, target, part_send.at[stage, p], part_recv.at[stage, p], **at(device))

    def wait_part(stage, p, ref):
        w = over(stage, p, ref, ref, me)
        w.wait_recv()
        w.wait_send()

    for p in range(3):
        other = pl.ds(pl.multiple_of((1 - me % 2) * 128, 128), 128)
        over(0, p, sums[p].at[other], pair[p], me ^ 1).start()

    x = me // BLOCK

    def send_block(source, target, send_at, recv_at, shift, to):
        pltpu.make_async_remote_copy(
            source.at[pl.ds(to * OWN, OWN)], target.at[pl.ds(shift + me * OWN, OWN)], send_at, recv_at, **at(to)
        ).start()

    def wait_blocks(n, semaphore):
        some = recv.at[pl.ds(0, n * OWN)]
        return pltpu.make_async_remote_copy(some, some, semaphore, semaphore, **at(me))

    for i in range(DEVICES - 1, 0, -1):
        send_block(send, recv, send_sem.at[0], recv_sem.at[i // BLOCK], PAD, me ^ i)
    own = pltpu.make_async_copy(
        send.at[pl.ds(me * OWN, OWN)], recv.at[pl.ds(PAD + me * OWN, OWN)], own_sem.at[0]
    )
    own.start()

    for p, (first, tiles, bit, _) in enumerate(PARTS):
        wait_part(0, p, pair[p])
        mine = pl.ds(pl.multiple_of((me % 2) * 128, 128), 128)
        chip[p][...] = sums[p][mine, :] + pair[p][...]
        for d in range(1, 4):
            to = me ^ (d << bit)
            block = pl.ds(pl.multiple_of(digit(to, bit) * 32, 32), 32)
            over(1, p, chip[p].at[block], first_in[p].at[pl.ds((d - 1) * 32, 32)], to).start()

    for c in loads[6:]:
        c.wait()
    prepare(cx, cy, nb, axa, aya, axb, ayb)

    def propagate(block):
        advect(block, recv, back, axa, aya, axb, ayb)
        for i in range(BLOCK - 1, 0, -1):
            send_block(back, out, send_sem.at[1], recv_sem.at[4], 0, block * BLOCK + (me % BLOCK) ^ i)

    half = x // 2
    wait_blocks(BLOCK, recv_sem.at[3]).wait_recv()
    wait_blocks(BLOCK, recv_sem.at[2]).wait_recv()
    propagate(3 * (1 - half))
    send_block(back, out, send_sem.at[1], recv_sem.at[4], 0, 3 * (1 - half) * BLOCK + me % BLOCK)
    wait_blocks(BLOCK, recv_sem.at[1]).wait_recv()
    own.wait()
    wait_blocks(BLOCK - 1, recv_sem.at[0]).wait_recv()
    own2 = pltpu.make_async_copy(back.at[pl.ds(me * OWN, OWN)], out.at[pl.ds(me * OWN, OWN)], own_sem.at[1])

    def two(b, carry):
        block = (1 - b) * (2 - half) + b * (x + 1 - 2 * (x % 2))
        propagate(block)
        send_block(back, out, send_sem.at[1], recv_sem.at[4], 0, block * BLOCK + me % BLOCK)
        return carry

    lax.fori_loop(0, 2, two, 0)
    for p, (first, tiles, bit, (b1, b2)) in enumerate(PARTS):
        wait_part(1, p, first_in[p])
        block = pl.ds(pl.multiple_of(digit(me, bit) * 32, 32), 32)
        for t in range(4):
            if t < tiles:
                lanes = slice(t * WIDTH, (t + 1) * WIDTH)
                v = chip[p][block, lanes]
                for d in range(3):
                    v = v + first_in[p][d * 32 : (d + 1) * 32, lanes]
            else:
                v = jnp.zeros((32, WIDTH), F32)
            second_out[p][pl.ds(t, 32, stride=4), :] = v

        mine = digit(me, b1) * 4 + digit(me, b2)
        for q in range(15, 0, -1):
            over(
                2,
                p,
                second_out[p].at[pl.ds(pl.multiple_of((mine ^ q) * 8, 8), 8)],
                second_in[p].at[pl.ds(q * 8, 8)],
                me ^ (((q >> 2) << b1) | ((q & 3) << b2)),
            ).start()
    propagate(x)
    own2.start()
    lane = lax.broadcasted_iota(jnp.int32, (WIDTH, WIDTH), 1)
    for p, (first, tiles, bit, (b1, b2)) in enumerate(PARTS):
        wait_part(2, p, second_in[p].at[pl.ds(8, 120)])
        block = digit(me, b1) * 4 + digit(me, b2)
        v = second_out[p][pl.ds(pl.multiple_of(block * 8, 8), 8), :]
        for q in range(1, 16):
            v = v + second_in[p][pl.ds(8 * q, 8), :]
        columns = v.T
        for t in range(tiles):
            if first + t < COMPS // WIDTH:
                added[pl.ds((first + t) * WIDTH, WIDTH), :] = jnp.where(
                    lane == 0, columns[:, t : t + 1], jnp.where(lane == WIDTH - 1, columns[:, 4 + t : 5 + t], 0.0)
                )
            else:
                one = lax.broadcasted_iota(jnp.int32, (8, WIDTH), 1)
                total = jnp.where(one == 0, v[t : t + 1], jnp.where(one == WIDTH - 1, v[4 + t : 5 + t], 0.0))
                scale[...] = 1.0 / (1.0 + total)
    wait_blocks(DEVICES - 1, send_sem.at[0]).wait_send()
    own2.wait()
    wait_blocks(DEVICES - 1, send_sem.at[1]).wait_send()
    wait_blocks(DEVICES - 1, recv_sem.at[4]).wait_recv()


def timestep(*arrays):
    whole = [pltpu.VMEM(a.shape, a.dtype) for a in arrays]
    anywhere = pl.BlockSpec(memory_space=pl.ANY)

    def rows(n):
        return pltpu.VMEM((n, WIDTH), F32)

    def parts(n):
        return [pltpu.VMEM((n, tiles * WIDTH), F32) for _, tiles, _, _ in PARTS]

    return pl.pallas_call(
        kernel,
        out_shape=(rows(COMPS), rows(COMPS), rows(8)),
        in_specs=[anywhere] * 9,
        out_specs=(pl.BlockSpec(memory_space=pltpu.VMEM),) * 3,
        scratch_shapes=[
            *whole,
            rows(8 * NTH),
            rows(COMPS),
            rows(PAD + COMPS + PAD),
            rows(COMPS),
            rows(8 * (DEVICES + 4)),
            rows(8 * (DEVICES + 4)),
            rows(DEVICES + 16),
            rows(DEVICES + 16),
            *parts(256),
            *parts(128),
            *parts(128),
            *parts(96),
            *[rows(128) for _ in PARTS],
            *[rows(128) for _ in PARTS],
            DMA((9,)),
            DMA((2,)),
            DMA((2,)),
            DMA((5,)),
            DMA((3, 3)),
            DMA((3, 3)),
        ],
        name="timestep",
        compiler_params=pltpu.CompilerParams(
            collective_id=1, has_side_effects=True, vmem_limit_bytes=60 * 1024 * 1024
        ),
    )(*arrays)


def body(spectrum, turning, courant_x, courant_y, neighbors, nest_spectra, nest_owner, nest_point, nest_weight):
    rows = nest_spectra.shape[0]
    energy, added, scale = timestep(
        spectrum,
        turning,
        courant_x,
        courant_y,
        neighbors,
        nest_spectra,
        nest_owner.reshape(1, rows),
        nest_point.reshape(1, rows),
        nest_weight.reshape(1, rows),
    )
    return (energy + added) * scale[0:1, :]


def solution(mesh):
    placed = (
        P(None, ("pts", "comp")),
        P(None, ("pts", "comp")),
        P(("pts", "comp"), None),
        P(("pts", "comp"), None),
        P(),
        P(("pts", "comp"), None),
        P(("pts", "comp"), None),
        P(("pts", "comp")),
        P(("pts", "comp")),
    )
    return jax.shard_map(body, mesh=mesh, in_specs=placed, out_specs=P(None, ("pts", "comp")), check_vma=False)
```

```python
import functools

import jax
import jax.numpy as jnp
from jax import lax
from jax.experimental import pallas as pl
from jax.experimental.pallas import tpu as pltpu
from jax.sharding import PartitionSpec as P

MESH = pl.DeviceIdType.MESH
DMA = pltpu.SemaphoreType.DMA
F32 = jnp.float32
BF16 = jnp.bfloat16
NTH = 36
DEVICES = 128
WIDTH = 128
COMPS = 1152
OWN = 9
PAD = 80
BLOCK = 32
PARTS = ((0, 4, 5, (3, 1)), (4, 3, 1, (5, 3)), (7, 3, 3, (5, 1)))


def at(device):
    return dict(device_id=(device // 8, device % 8), device_id_type=MESH)


def digit(index, bit):
    return (index >> bit) & 3


def refract(x, r, tmp, send):
    @pl.loop(0, x.shape[0] // (8 * NTH))
    def _(group):
        base = pl.multiple_of(group * (8 * NTH), 8)

        def substep(load, store):
            def flux(d):
                rate = r[pl.ds(base + d, 8, stride=NTH), :]
                return jnp.maximum(rate, 0.0) * load(d) + jnp.minimum(rate, 0.0) * load((d + 1) % NTH)

            before = flux(NTH - 1)
            for d in range(NTH):
                now = flux(d)
                store(d, load(d) - now + before)
                before = now

        def load_x(d):
            return x[pl.ds(base + d, 8, stride=NTH), :]

        def store_tmp(d, v):
            tmp[pl.ds(8 * d, 8), :] = v

        def load_tmp(d):
            return tmp[pl.ds(8 * d, 8), :]

        def store_send(d, v):
            send[pl.ds(base + d, 8, stride=NTH), :] = v

        substep(load_x, store_tmp)
        substep(load_tmp, store_send)


def local_sums(spectra, owner, point, weight, sums):
    rows = spectra.shape[0]
    w = weight[...]
    diagonal = lax.broadcasted_iota(jnp.int32, (rows, rows), 0) == lax.broadcasted_iota(jnp.int32, (rows, rows), 1)
    w_column = jnp.sum(jnp.where(diagonal, w, 0.0), axis=1, keepdims=True)
    o = owner[...]
    end = (point[...] > 0).astype(jnp.int32)
    place = lax.broadcasted_iota(jnp.int32, (256, rows), 0)
    for (first, tiles, bit, (b1, b2)), out in zip(PARTS, sums):
        target = (o & 1) * 128 + digit(o, bit) * 32 + digit(o, b1) * 8 + digit(o, b2) * 2 + end
        table = (place == target).astype(F32).astype(BF16)
        for t in range(tiles):
            if first + t < COMPS // WIDTH:
                v = spectra[:, (first + t) * WIDTH : (first + t + 1) * WIDTH] * w_column
            else:
                v = jnp.broadcast_to(w_column, (rows, WIDTH))
            high = v.astype(BF16)
            low = (v - high.astype(F32)).astype(BF16)
            out[:, t * WIDTH : (t + 1) * WIDTH] = jnp.dot(table, high, preferred_element_type=F32) + jnp.dot(
                table, low, preferred_element_type=F32
            )


def prepare(cx, cy, nb, axa, aya, axb, ayb):
    lane = lax.broadcasted_iota(jnp.int32, (4, WIDTH), 1)
    side = lax.broadcasted_iota(jnp.int32, (4, WIDTH), 0)
    shift = lane + jnp.where(side == 0, -1, jnp.where(side == 1, 1, jnp.where(side == 2, -WIDTH, WIDTH)))
    for a, edge in ((axa, 16), (aya, 16), (axb, 8), (ayb, 8)):
        a[pl.ds(0, edge), :] = jnp.zeros((edge, WIDTH), F32)
        a[pl.ds(a.shape[0] - edge, edge), :] = jnp.zeros((edge, WIDTH), F32)

    @pl.loop(0, DEVICES // 8)
    def _(group):
        for j in range(8):
            s = group * 8 + j
            columns = pl.ds(pl.multiple_of(s * WIDTH, WIDTH), WIDTH)
            there = (nb[:, columns] == shift + s * WIDTH).astype(F32)
            for c, a, b, low in ((cx, axa, axb, 0), (cy, aya, ayb, 2)):
                up, down = there[low : low + 1], there[low + 1 : low + 2]
                v = c[pl.ds(0, 8), columns]
                a[pl.ds(pl.multiple_of((s + 2) * 8, 8), 8), :] = v * jnp.where(v > 0, up, down)
                v = c[pl.ds(8, 1), columns]
                b[pl.ds(pl.multiple_of(group * 8, 8) + (8 + j), 1), :] = v * jnp.where(v > 0, up, down)


def upwind(e, south, north, vx, vy):
    west, east = pltpu.roll(e, 1, 1), pltpu.roll(e, WIDTH - 1, 1)
    out = e - jnp.abs(vx) * (e - jnp.where(vx > 0, west, east))
    return out - jnp.abs(vy) * (e - jnp.where(vy > 0, south, north))


def advect(block, recv, back, axa, aya, axb, ayb):
    base = pl.multiple_of(block * (BLOCK * OWN), 8)
    low = pl.multiple_of(block * (BLOCK * 8), 8)

    def courants(s):
        rows = pl.ds(low + 8 * (s + 2), 8)
        return axa[rows, :], aya[rows, :]

    def first(s):
        return recv[pl.ds(base + (PAD + OWN * s), 8), :]

    e0, e1, e2, c = {-3: first(-3), -2: first(-2)}, {}, {}, {}
    for s in range(-2, BLOCK + 2):
        e0[s + 1], c[s] = first(s + 1), courants(s)
        e1[s] = upwind(e0[s], e0[s - 1], e0[s + 1], *c[s])
        if s >= 0:
            e2[s - 1] = upwind(e1[s - 1], e1[s - 2], e1[s], *c[s - 1])
        if s >= 2:
            back[pl.ds(base + OWN * (s - 2), 8), :] = upwind(e2[s - 2], e2[s - 3], e2[s - 1], *c[s - 2])
    groups = BLOCK // 8 + 2
    last = groups - 1
    e = [recv[pl.ds(base + (PAD + 8 + 72 * (g - 1)), 8, stride=OWN), :] for g in range(groups)]
    courant = pl.multiple_of(block * BLOCK, 8)
    row = lax.broadcasted_iota(jnp.int32, (8, WIDTH), 0)
    for _ in range(3):
        up = [pltpu.roll(v, 1, 0) for v in e]
        down = [pltpu.roll(v, 7, 0) for v in e]
        e = [
            upwind(
                e[g],
                jnp.where(row == 0, up[max(g - 1, 0)], up[g]),
                jnp.where(row == 7, down[min(g + 1, last)], down[g]),
                axb[pl.ds(courant + 8 * g, 8), :],
                ayb[pl.ds(courant + 8 * g, 8), :],
            )
            for g in range(groups)
        ]
    for g in range(1, last):
        back[pl.ds(base + (8 + 72 * (g - 1)), 8, stride=OWN), :] = e[g]


def kernel(
    x_hbm, r_hbm, cx_hbm, cy_hbm, nb_hbm, ns_hbm, owner_hbm, point_hbm, weight_hbm, out, added, scale, *scratch
):
    spec, r, cx, cy, nb, ns, owner, point, weight = scratch[:9]
    tmp, send, recv, back, axa, aya, axb, ayb = scratch[9:17]
    sums, pair, chip, first_in, second_out, second_in = (scratch[17 + 3 * i : 20 + 3 * i] for i in range(6))
    in_sem, own_sem, send_sem, recv_sem, part_send, part_recv = scratch[35:]
    me = lax.axis_index("pts") * 8 + lax.axis_index("comp")
    loads = [
        pltpu.make_async_copy(a, b, in_sem.at[i])
        for i, (a, b) in enumerate(
            (
                (x_hbm, spec),
                (r_hbm, r),
                (ns_hbm, ns),
                (owner_hbm, owner),
                (point_hbm, point),
                (weight_hbm, weight),
                (cx_hbm, cx),
                (cy_hbm, cy),
                (nb_hbm, nb),
            )
        )
    ]
    for c in loads[:2]:
        c.start()
    barrier = pltpu.get_barrier_semaphore()
    for i in range(DEVICES - 1, 0, -1):
        pl.semaphore_signal(barrier, inc=1, **at(me ^ i))

    for c in loads[2:]:
        c.start()
    recv[pl.ds(0, PAD), :] = jnp.zeros((PAD, WIDTH), F32)
    recv[pl.ds(PAD + COMPS, PAD), :] = jnp.zeros((PAD, WIDTH), F32)
    loads[0].wait()
    loads[1].wait()
    refract(spec, r, tmp, send)
    pl.semaphore_wait(barrier, DEVICES - 1)

    def over(stage, p, source, target, device):
        return pltpu.make_async_remote_copy(source, target, part_send.at[stage, p], part_recv.at[stage, p], **at(device))

    def wait_part(stage, p, ref):
        w = over(stage, p, ref, ref, me)
        w.wait_recv()
        w.wait_send()

    x = me // BLOCK

    def send_block(source, target, send_at, recv_at, shift, to):
        pltpu.make_async_remote_copy(
            source.at[pl.ds(to * OWN, OWN)], target.at[pl.ds(shift + me * OWN, OWN)], send_at, recv_at, **at(to)
        ).start()

    def wait_blocks(n, semaphore):
        some = recv.at[pl.ds(0, n * OWN)]
        return pltpu.make_async_remote_copy(some, some, semaphore, semaphore, **at(me))

    for i in range(DEVICES - 1, 0, -1):
        send_block(send, recv, send_sem.at[0], recv_sem.at[i // BLOCK], PAD, me ^ i)
    own = pltpu.make_async_copy(
        send.at[pl.ds(me * OWN, OWN)], recv.at[pl.ds(PAD + me * OWN, OWN)], own_sem.at[0]
    )
    own.start()

    for c in loads[2:6]:
        c.wait()
    local_sums(ns, owner, point, weight, sums)
    for p in range(3):
        other = pl.ds(pl.multiple_of((1 - me % 2) * 128, 128), 128)
        over(0, p, sums[p].at[other], pair[p], me ^ 1).start()

    for p, (first, tiles, bit, _) in enumerate(PARTS):
        wait_part(0, p, pair[p])
        mine = pl.ds(pl.multiple_of((me % 2) * 128, 128), 128)
        chip[p][...] = sums[p][mine, :] + pair[p][...]
        for d in range(1, 4):
            to = me ^ (d << bit)
            block = pl.ds(pl.multiple_of(digit(to, bit) * 32, 32), 32)
            over(1, p, chip[p].at[block], first_in[p].at[pl.ds((d - 1) * 32, 32)], to).start()

    for c in loads[6:]:
        c.wait()
    prepare(cx, cy, nb, axa, aya, axb, ayb)

    def propagate(block):
        advect(block, recv, back, axa, aya, axb, ayb)
        for i in range(BLOCK - 1, 0, -1):
            send_block(back, out, send_sem.at[1], recv_sem.at[4], 0, block * BLOCK + (me % BLOCK) ^ i)

    half = x // 2
    wait_blocks(BLOCK, recv_sem.at[3]).wait_recv()
    wait_blocks(BLOCK, recv_sem.at[2]).wait_recv()
    propagate(3 * (1 - half))
    send_block(back, out, send_sem.at[1], recv_sem.at[4], 0, 3 * (1 - half) * BLOCK + me % BLOCK)
    wait_blocks(BLOCK, recv_sem.at[1]).wait_recv()
    own.wait()
    wait_blocks(BLOCK - 1, recv_sem.at[0]).wait_recv()
    own2 = pltpu.make_async_copy(back.at[pl.ds(me * OWN, OWN)], out.at[pl.ds(me * OWN, OWN)], own_sem.at[1])

    def two(b, carry):
        block = (1 - b) * (2 - half) + b * (x + 1 - 2 * (x % 2))
        propagate(block)
        send_block(back, out, send_sem.at[1], recv_sem.at[4], 0, block * BLOCK + me % BLOCK)
        return carry

    lax.fori_loop(0, 2, two, 0)
    for p, (first, tiles, bit, (b1, b2)) in enumerate(PARTS):
        wait_part(1, p, first_in[p])
        block = pl.ds(pl.multiple_of(digit(me, bit) * 32, 32), 32)
        for t in range(4):
            if t < tiles:
                lanes = slice(t * WIDTH, (t + 1) * WIDTH)
                v = chip[p][block, lanes]
                for d in range(3):
                    v = v + first_in[p][d * 32 : (d + 1) * 32, lanes]
            else:
                v = jnp.zeros((32, WIDTH), F32)
            second_out[p][pl.ds(t, 32, stride=4), :] = v

        mine = digit(me, b1) * 4 + digit(me, b2)
        for q in range(15, 0, -1):
            over(
                2,
                p,
                second_out[p].at[pl.ds(pl.multiple_of((mine ^ q) * 8, 8), 8)],
                second_in[p].at[pl.ds(q * 8, 8)],
                me ^ (((q >> 2) << b1) | ((q & 3) << b2)),
            ).start()
    propagate(x)
    own2.start()
    lane = lax.broadcasted_iota(jnp.int32, (WIDTH, WIDTH), 1)
    for p, (first, tiles, bit, (b1, b2)) in enumerate(PARTS):
        wait_part(2, p, second_in[p].at[pl.ds(8, 120)])
        block = digit(me, b1) * 4 + digit(me, b2)
        v = second_out[p][pl.ds(pl.multiple_of(block * 8, 8), 8), :]
        for q in range(1, 16):
            v = v + second_in[p][pl.ds(8 * q, 8), :]
        columns = v.T
        for t in range(tiles):
            if first + t < COMPS // WIDTH:
                added[pl.ds((first + t) * WIDTH, WIDTH), :] = jnp.where(
                    lane == 0, columns[:, t : t + 1], jnp.where(lane == WIDTH - 1, columns[:, 4 + t : 5 + t], 0.0)
                )
            else:
                one = lax.broadcasted_iota(jnp.int32, (8, WIDTH), 1)
                total = jnp.where(one == 0, v[t : t + 1], jnp.where(one == WIDTH - 1, v[4 + t : 5 + t], 0.0))
                scale[...] = 1.0 / (1.0 + total)
    wait_blocks(DEVICES - 1, send_sem.at[0]).wait_send()
    own2.wait()
    wait_blocks(DEVICES - 1, send_sem.at[1]).wait_send()
    wait_blocks(DEVICES - 1, recv_sem.at[4]).wait_recv()


def timestep(*arrays):
    whole = [pltpu.VMEM(a.shape, a.dtype) for a in arrays]
    anywhere = pl.BlockSpec(memory_space=pl.ANY)

    def rows(n):
        return pltpu.VMEM((n, WIDTH), F32)

    def parts(n):
        return [pltpu.VMEM((n, tiles * WIDTH), F32) for _, tiles, _, _ in PARTS]

    return pl.pallas_call(
        kernel,
        out_shape=(rows(COMPS), rows(COMPS), rows(8)),
        in_specs=[anywhere] * 9,
        out_specs=(pl.BlockSpec(memory_space=pltpu.VMEM),) * 3,
        scratch_shapes=[
            *whole,
            rows(8 * NTH),
            rows(COMPS),
            rows(PAD + COMPS + PAD),
            rows(COMPS),
            rows(8 * (DEVICES + 4)),
            rows(8 * (DEVICES + 4)),
            rows(DEVICES + 16),
            rows(DEVICES + 16),
            *parts(256),
            *parts(128),
            *parts(128),
            *parts(96),
            *[rows(128) for _ in PARTS],
            *[rows(128) for _ in PARTS],
            DMA((9,)),
            DMA((2,)),
            DMA((2,)),
            DMA((5,)),
            DMA((3, 3)),
            DMA((3, 3)),
        ],
        name="timestep",
        compiler_params=pltpu.CompilerParams(
            collective_id=1, has_side_effects=True, vmem_limit_bytes=60 * 1024 * 1024
        ),
    )(*arrays)


def body(spectrum, turning, courant_x, courant_y, neighbors, nest_spectra, nest_owner, nest_point, nest_weight):
    rows = nest_spectra.shape[0]
    energy, added, scale = timestep(
        spectrum,
        turning,
        courant_x,
        courant_y,
        neighbors,
        nest_spectra,
        nest_owner.reshape(1, rows),
        nest_point.reshape(1, rows),
        nest_weight.reshape(1, rows),
    )
    return (energy + added) * scale[0:1, :]


def solution(mesh):
    placed = (
        P(None, ("pts", "comp")),
        P(None, ("pts", "comp")),
        P(("pts", "comp"), None),
        P(("pts", "comp"), None),
        P(),
        P(("pts", "comp"), None),
        P(("pts", "comp"), None),
        P(("pts", "comp")),
        P(("pts", "comp")),
    )
    return jax.shard_map(body, mesh=mesh, in_specs=placed, out_specs=P(None, ("pts", "comp")), check_vma=False)
```

```python
import functools

import jax
import jax.numpy as jnp
from jax import lax
from jax.experimental import pallas as pl
from jax.experimental.pallas import tpu as pltpu
from jax.sharding import PartitionSpec as P

MESH = pl.DeviceIdType.MESH
DMA = pltpu.SemaphoreType.DMA
F32 = jnp.float32
BF16 = jnp.bfloat16
NTH = 36
DEVICES = 128
WIDTH = 128
COMPS = 1152
OWN = 9
PAD = 80
BLOCK = 32
PARTS = ((0, 4, 5, (3, 1)), (4, 3, 1, (5, 3)), (7, 3, 3, (5, 1)))


def at(device):
    return dict(device_id=(device // 8, device % 8), device_id_type=MESH)


def digit(index, bit):
    return (index >> bit) & 3


def hops(i):
    return sum(min(digit(i, bit), 4 - digit(i, bit)) for bit in (1, 3, 5))


def refract(x, r, tmp, send):
    @pl.loop(0, x.shape[0] // (8 * NTH))
    def _(group):
        base = pl.multiple_of(group * (8 * NTH), 8)

        def substep(load, store):
            def flux(d):
                rate = r[pl.ds(base + d, 8, stride=NTH), :]
                return jnp.maximum(rate, 0.0) * load(d) + jnp.minimum(rate, 0.0) * load((d + 1) % NTH)

            before = flux(NTH - 1)
            for d in range(NTH):
                now = flux(d)
                store(d, load(d) - now + before)
                before = now

        def load_x(d):
            return x[pl.ds(base + d, 8, stride=NTH), :]

        def store_tmp(d, v):
            tmp[pl.ds(8 * d, 8), :] = v

        def load_tmp(d):
            return tmp[pl.ds(8 * d, 8), :]

        def store_send(d, v):
            send[pl.ds(base + d, 8, stride=NTH), :] = v

        substep(load_x, store_tmp)
        substep(load_tmp, store_send)


def local_sums(spectra, owner, point, weight, sums):
    rows = spectra.shape[0]
    w = weight[...]
    diagonal = lax.broadcasted_iota(jnp.int32, (rows, rows), 0) == lax.broadcasted_iota(jnp.int32, (rows, rows), 1)
    w_column = jnp.sum(jnp.where(diagonal, w, 0.0), axis=1, keepdims=True)
    o = owner[...]
    end = (point[...] > 0).astype(jnp.int32)
    place = lax.broadcasted_iota(jnp.int32, (256, rows), 0)
    for (first, tiles, bit, (b1, b2)), out in zip(PARTS, sums):
        target = (o & 1) * 128 + digit(o, bit) * 32 + digit(o, b1) * 8 + digit(o, b2) * 2 + end
        table = (place == target).astype(F32).astype(BF16)
        for t in range(tiles):
            if first + t < COMPS // WIDTH:
                v = spectra[:, (first + t) * WIDTH : (first + t + 1) * WIDTH] * w_column
            else:
                v = jnp.broadcast_to(w_column, (rows, WIDTH))
            high = v.astype(BF16)
            low = (v - high.astype(F32)).astype(BF16)
            out[:, t * WIDTH : (t + 1) * WIDTH] = jnp.dot(table, high, preferred_element_type=F32) + jnp.dot(
                table, low, preferred_element_type=F32
            )


def prepare(cx, cy, nb, axa, aya, axb, ayb):
    lane = lax.broadcasted_iota(jnp.int32, (4, WIDTH), 1)
    side = lax.broadcasted_iota(jnp.int32, (4, WIDTH), 0)
    shift = lane + jnp.where(side == 0, -1, jnp.where(side == 1, 1, jnp.where(side == 2, -WIDTH, WIDTH)))
    for a, edge in ((axa, 16), (aya, 16), (axb, 8), (ayb, 8)):
        a[pl.ds(0, edge), :] = jnp.zeros((edge, WIDTH), F32)
        a[pl.ds(a.shape[0] - edge, edge), :] = jnp.zeros((edge, WIDTH), F32)

    @pl.loop(0, DEVICES // 8)
    def _(group):
        for j in range(8):
            s = group * 8 + j
            columns = pl.ds(pl.multiple_of(s * WIDTH, WIDTH), WIDTH)
            there = (nb[:, columns] == shift + s * WIDTH).astype(F32)
            for c, a, b, low in ((cx, axa, axb, 0), (cy, aya, ayb, 2)):
                up, down = there[low : low + 1], there[low + 1 : low + 2]
                v = c[pl.ds(0, 8), columns]
                a[pl.ds(pl.multiple_of((s + 2) * 8, 8), 8), :] = v * jnp.where(v > 0, up, down)
                v = c[pl.ds(8, 1), columns]
                b[pl.ds(pl.multiple_of(group * 8, 8) + (8 + j), 1), :] = v * jnp.where(v > 0, up, down)


def upwind(e, south, north, vx, vy):
    west, east = pltpu.roll(e, 1, 1), pltpu.roll(e, WIDTH - 1, 1)
    out = e - jnp.abs(vx) * (e - jnp.where(vx > 0, west, east))
    return out - jnp.abs(vy) * (e - jnp.where(vy > 0, south, north))


def advect(block, recv, back, axa, aya, axb, ayb):
    base = pl.multiple_of(block * (BLOCK * OWN), 8)
    low = pl.multiple_of(block * (BLOCK * 8), 8)

    def courants(s):
        rows = pl.ds(low + 8 * (s + 2), 8)
        return axa[rows, :], aya[rows, :]

    def first(s):
        return recv[pl.ds(base + (PAD + OWN * s), 8), :]

    e0, e1, e2, c = {-3: first(-3), -2: first(-2)}, {}, {}, {}
    for s in range(-2, BLOCK + 2):
        e0[s + 1], c[s] = first(s + 1), courants(s)
        e1[s] = upwind(e0[s], e0[s - 1], e0[s + 1], *c[s])
        if s >= 0:
            e2[s - 1] = upwind(e1[s - 1], e1[s - 2], e1[s], *c[s - 1])
        if s >= 2:
            back[pl.ds(base + OWN * (s - 2), 8), :] = upwind(e2[s - 2], e2[s - 3], e2[s - 1], *c[s - 2])
    groups = BLOCK // 8 + 2
    last = groups - 1
    e = [recv[pl.ds(base + (PAD + 8 + 72 * (g - 1)), 8, stride=OWN), :] for g in range(groups)]
    courant = pl.multiple_of(block * BLOCK, 8)
    row = lax.broadcasted_iota(jnp.int32, (8, WIDTH), 0)
    for _ in range(3):
        up = [pltpu.roll(v, 1, 0) for v in e]
        down = [pltpu.roll(v, 7, 0) for v in e]
        e = [
            upwind(
                e[g],
                jnp.where(row == 0, up[max(g - 1, 0)], up[g]),
                jnp.where(row == 7, down[min(g + 1, last)], down[g]),
                axb[pl.ds(courant + 8 * g, 8), :],
                ayb[pl.ds(courant + 8 * g, 8), :],
            )
            for g in range(groups)
        ]
    for g in range(1, last):
        back[pl.ds(base + (8 + 72 * (g - 1)), 8, stride=OWN), :] = e[g]


def kernel(
    x_hbm, r_hbm, cx_hbm, cy_hbm, nb_hbm, ns_hbm, owner_hbm, point_hbm, weight_hbm, out, added, scale, *scratch
):
    spec, r, cx, cy, nb, ns, owner, point, weight = scratch[:9]
    tmp, send, recv, back, axa, aya, axb, ayb = scratch[9:17]
    sums, pair, chip, first_in, second_out, second_in = (scratch[17 + 3 * i : 20 + 3 * i] for i in range(6))
    in_sem, own_sem, send_sem, recv_sem, part_send, part_recv = scratch[35:]
    me = lax.axis_index("pts") * 8 + lax.axis_index("comp")
    loads = [
        pltpu.make_async_copy(a, b, in_sem.at[i])
        for i, (a, b) in enumerate(
            (
                (x_hbm, spec),
                (r_hbm, r),
                (ns_hbm, ns),
                (owner_hbm, owner),
                (point_hbm, point),
                (weight_hbm, weight),
                (cx_hbm, cx),
                (cy_hbm, cy),
                (nb_hbm, nb),
            )
        )
    ]
    for c in loads:
        c.start()
    barrier = pltpu.get_barrier_semaphore()
    for i in range(DEVICES - 1, 0, -1):
        pl.semaphore_signal(barrier, inc=1, **at(me ^ i))

    recv[pl.ds(0, PAD), :] = jnp.zeros((PAD, WIDTH), F32)
    recv[pl.ds(PAD + COMPS, PAD), :] = jnp.zeros((PAD, WIDTH), F32)
    loads[0].wait()
    loads[1].wait()
    refract(spec, r, tmp, send)
    for c in loads[2:6]:
        c.wait()
    local_sums(ns, owner, point, weight, sums)
    pl.semaphore_wait(barrier, DEVICES - 1)

    def over(stage, p, source, target, device):
        return pltpu.make_async_remote_copy(source, target, part_send.at[stage, p], part_recv.at[stage, p], **at(device))

    def wait_part(stage, p, ref):
        w = over(stage, p, ref, ref, me)
        w.wait_recv()
        w.wait_send()

    for p in range(3):
        other = pl.ds(pl.multiple_of((1 - me % 2) * 128, 128), 128)
        over(0, p, sums[p].at[other], pair[p], me ^ 1).start()

    x = me // BLOCK

    def send_block(source, target, send_at, recv_at, shift, to):
        pltpu.make_async_remote_copy(
            source.at[pl.ds(to * OWN, OWN)], target.at[pl.ds(shift + me * OWN, OWN)], send_at, recv_at, **at(to)
        ).start()

    def wait_blocks(n, semaphore):
        some = recv.at[pl.ds(0, n * OWN)]
        return pltpu.make_async_remote_copy(some, some, semaphore, semaphore, **at(me))

    for i in sorted(range(1, DEVICES), key=lambda i: (-(i // BLOCK), -hops(i), -i)):
        send_block(send, recv, send_sem.at[0], recv_sem.at[i // BLOCK], PAD, me ^ i)
    own = pltpu.make_async_copy(
        send.at[pl.ds(me * OWN, OWN)], recv.at[pl.ds(PAD + me * OWN, OWN)], own_sem.at[0]
    )
    own.start()

    for p, (first, tiles, bit, _) in enumerate(PARTS):
        wait_part(0, p, pair[p])
        mine = pl.ds(pl.multiple_of((me % 2) * 128, 128), 128)
        chip[p][...] = sums[p][mine, :] + pair[p][...]
        for d in range(1, 4):
            to = me ^ (d << bit)
            block = pl.ds(pl.multiple_of(digit(to, bit) * 32, 32), 32)
            over(1, p, chip[p].at[block], first_in[p].at[pl.ds((d - 1) * 32, 32)], to).start()

    for c in loads[6:]:
        c.wait()
    prepare(cx, cy, nb, axa, aya, axb, ayb)

    def propagate(block):
        advect(block, recv, back, axa, aya, axb, ayb)
        for i in range(BLOCK - 1, 0, -1):
            send_block(back, out, send_sem.at[1], recv_sem.at[4], 0, block * BLOCK + (me % BLOCK) ^ i)

    half = x // 2
    wait_blocks(BLOCK, recv_sem.at[3]).wait_recv()
    wait_blocks(BLOCK, recv_sem.at[2]).wait_recv()
    propagate(3 * (1 - half))
    send_block(back, out, send_sem.at[1], recv_sem.at[4], 0, 3 * (1 - half) * BLOCK + me % BLOCK)
    wait_blocks(BLOCK, recv_sem.at[1]).wait_recv()
    own.wait()
    wait_blocks(BLOCK - 1, recv_sem.at[0]).wait_recv()
    own2 = pltpu.make_async_copy(back.at[pl.ds(me * OWN, OWN)], out.at[pl.ds(me * OWN, OWN)], own_sem.at[1])

    def two(b, carry):
        block = (1 - b) * (2 - half) + b * (x + 1 - 2 * (x % 2))
        propagate(block)
        send_block(back, out, send_sem.at[1], recv_sem.at[4], 0, block * BLOCK + me % BLOCK)
        return carry

    lax.fori_loop(0, 2, two, 0)
    for p, (first, tiles, bit, (b1, b2)) in enumerate(PARTS):
        wait_part(1, p, first_in[p])
        block = pl.ds(pl.multiple_of(digit(me, bit) * 32, 32), 32)
        for t in range(4):
            if t < tiles:
                lanes = slice(t * WIDTH, (t + 1) * WIDTH)
                v = chip[p][block, lanes]
                for d in range(3):
                    v = v + first_in[p][d * 32 : (d + 1) * 32, lanes]
            else:
                v = jnp.zeros((32, WIDTH), F32)
            second_out[p][pl.ds(t, 32, stride=4), :] = v

        mine = digit(me, b1) * 4 + digit(me, b2)
        for q in range(15, 0, -1):
            over(
                2,
                p,
                second_out[p].at[pl.ds(pl.multiple_of((mine ^ q) * 8, 8), 8)],
                second_in[p].at[pl.ds(q * 8, 8)],
                me ^ (((q >> 2) << b1) | ((q & 3) << b2)),
            ).start()
    propagate(x)
    own2.start()
    lane = lax.broadcasted_iota(jnp.int32, (WIDTH, WIDTH), 1)
    for p, (first, tiles, bit, (b1, b2)) in enumerate(PARTS):
        wait_part(2, p, second_in[p].at[pl.ds(8, 120)])
        block = digit(me, b1) * 4 + digit(me, b2)
        v = second_out[p][pl.ds(pl.multiple_of(block * 8, 8), 8), :]
        for q in range(1, 16):
            v = v + second_in[p][pl.ds(8 * q, 8), :]
        columns = v.T
        for t in range(tiles):
            if first + t < COMPS // WIDTH:
                added[pl.ds((first + t) * WIDTH, WIDTH), :] = jnp.where(
                    lane == 0, columns[:, t : t + 1], jnp.where(lane == WIDTH - 1, columns[:, 4 + t : 5 + t], 0.0)
                )
            else:
                one = lax.broadcasted_iota(jnp.int32, (8, WIDTH), 1)
                total = jnp.where(one == 0, v[t : t + 1], jnp.where(one == WIDTH - 1, v[4 + t : 5 + t], 0.0))
                scale[...] = 1.0 / (1.0 + total)
    wait_blocks(DEVICES - 1, send_sem.at[0]).wait_send()
    own2.wait()
    wait_blocks(DEVICES - 1, send_sem.at[1]).wait_send()
    wait_blocks(DEVICES - 1, recv_sem.at[4]).wait_recv()


def timestep(*arrays):
    whole = [pltpu.VMEM(a.shape, a.dtype) for a in arrays]
    anywhere = pl.BlockSpec(memory_space=pl.ANY)

    def rows(n):
        return pltpu.VMEM((n, WIDTH), F32)

    def parts(n):
        return [pltpu.VMEM((n, tiles * WIDTH), F32) for _, tiles, _, _ in PARTS]

    return pl.pallas_call(
        kernel,
        out_shape=(rows(COMPS), rows(COMPS), rows(8)),
        in_specs=[anywhere] * 9,
        out_specs=(pl.BlockSpec(memory_space=pltpu.VMEM),) * 3,
        scratch_shapes=[
            *whole,
            rows(8 * NTH),
            rows(COMPS),
            rows(PAD + COMPS + PAD),
            rows(COMPS),
            rows(8 * (DEVICES + 4)),
            rows(8 * (DEVICES + 4)),
            rows(DEVICES + 16),
            rows(DEVICES + 16),
            *parts(256),
            *parts(128),
            *parts(128),
            *parts(96),
            *[rows(128) for _ in PARTS],
            *[rows(128) for _ in PARTS],
            DMA((9,)),
            DMA((2,)),
            DMA((2,)),
            DMA((5,)),
            DMA((3, 3)),
            DMA((3, 3)),
        ],
        name="timestep",
        compiler_params=pltpu.CompilerParams(
            collective_id=1, has_side_effects=True, vmem_limit_bytes=60 * 1024 * 1024
        ),
    )(*arrays)


def body(spectrum, turning, courant_x, courant_y, neighbors, nest_spectra, nest_owner, nest_point, nest_weight):
    rows = nest_spectra.shape[0]
    energy, added, scale = timestep(
        spectrum,
        turning,
        courant_x,
        courant_y,
        neighbors,
        nest_spectra,
        nest_owner.reshape(1, rows),
        nest_point.reshape(1, rows),
        nest_weight.reshape(1, rows),
    )
    return (energy + added) * scale[0:1, :]


def solution(mesh):
    placed = (
        P(None, ("pts", "comp")),
        P(None, ("pts", "comp")),
        P(("pts", "comp"), None),
        P(("pts", "comp"), None),
        P(),
        P(("pts", "comp"), None),
        P(("pts", "comp"), None),
        P(("pts", "comp")),
        P(("pts", "comp")),
    )
    return jax.shard_map(body, mesh=mesh, in_specs=placed, out_specs=P(None, ("pts", "comp")), check_vma=False)
```
